512 devices in a mesh: gx: 8 (over x, z_hi), gy: 8 (over z_lo), gz: 8 (over y, core).
Axes of the slice: x: 4, y: 4, z: 16 (z_hi: 2, z_lo: 8; z = z_hi * 8 + z_lo), core: 2. Of those that a mesh axis runs over, the one named last changes fastest.
Arguments:
- positions: float32 [3, 32, 32, 16, 128], P(None, 'gx', 'gy', 'gz'), as said below
- volume: float32 [32, 32, 16, 128], P('gx', 'gy', 'gz'), may hold values from 0.5 to 2
- displacement: float32 [3, 32, 32, 16, 128], P(None, 'gx', 'gy', 'gz'), may hold values from -0.12 to 0.12
- velocity: float32 [3, 32, 32, 16, 128], P(None, 'gx', 'gy', 'gz'), may hold values from -1 to 1
- acceleration: float32 [3, 32, 32, 16, 128], P(None, 'gx', 'gy', 'gz'), may hold values from -4 to 4
- tile_own: int32 [8, 8, 8, 40], P('gx', 'gy', 'gz'), may hold values from 29 to 114, as said below
- tile_partner: int32 [8, 8, 8, 40], P('gx', 'gy', 'gz'), may hold values from 0 to 143, as said below
- tile_count: int32 [8, 8, 8], P('gx', 'gy', 'gz'), may hold values from 30 to 40, as said below
- family_bits: int32 [8, 8, 8, 40, 16, 128], P('gx', 'gy', 'gz'), may hold values from 0 to 255, as said below
- broken_bits: int32 [8, 8, 8, 40, 16, 128], P('gx', 'gy', 'gz'), may hold values from 0 to 255, as said below
Outputs:
- final_displacement: float32 [3, 32, 32, 16, 128], P(None, 'gx', 'gy', 'gz')
- final_velocity: float32 [3, 32, 32, 16, 128], P(None, 'gx', 'gy', 'gz')
- final_acceleration: float32 [3, 32, 32, 16, 128], P(None, 'gx', 'gy', 'gz')
The draws below stay inside these ranges and needn't reach their ends.
Inputs may be any that keep to these rules, and one draw needn't show every extreme that they name: `tile_own`: each entry names an interior block of the device's padded grid of (6) x (6) x (4) blocks, numbered row-major. `tile_partner`: each entry is tile_own of the same slot moved by one of the 27 block offsets (dx, dy, dz) with dx, dy, dz in -1, 0, 1. `tile_count`: each device uses 40 or 30 slots, the first ones; both counts occur. `family_bits`: eight bond bits a word, bit k of word w of row a for partner point 8 w + k. `broken_bits`: eight bond bits a word, laid out as family_bits. `positions`: each block holds a 4 x 4 x 8 lattice of points of spacing 1, block (i, j, k) starting at (4 i, 4 j, 8 k); every coordinate of a point lies within 0.2 of its lattice site's, 0.5 past the lower corner.
All inputs are finite; a program needn't handle non-finite values.
Results may differ from the reference program's by a relative error of at most 0.0003.
Values sent between devices are 32-bit elements; how exact they have to be, the bound alone decides.
A program may use at most 64 MiB of HBM per device.

```python
import math
import jax
import jax.numpy as jnp
import numpy as np
from jax import lax

BLK = 128
WORDS = 16
BX = 4
BY = 4
BZ = 2
TILES = 40
GROUP = 8
STEPS = 2
NBX = 32
NBY = 32
NBZ = 16
N_GX = 8
N_GY = 8
N_GZ = 8


FULL_SHELL = np.array([[a, b, c] for a in (-1, 0, 1) for b in (-1, 0, 1) for c in (-1, 0, 1)], dtype=np.int32)


def draw_positions(key, part):
    key = jax.random.fold_in(key, 11)
    jitter = jax.random.uniform(key, (3, NBX, NBY, NBZ, BLK), jnp.float32, -0.2, 0.2)
    point_index = jnp.arange(BLK, dtype=jnp.int32)
    site_x = jnp.arange(NBX, dtype=jnp.int32)[:, None, None, None] * 4 + (point_index // 32)[None, None, None, :]
    site_y = jnp.arange(NBY, dtype=jnp.int32)[None, :, None, None] * 4 + (point_index // 8 % 4)[None, None, None, :]
    site_z = jnp.arange(NBZ, dtype=jnp.int32)[None, None, :, None] * 8 + (point_index % 8)[None, None, None, :]
    full_shape = (NBX, NBY, NBZ, BLK)
    lattice = jnp.stack([jnp.broadcast_to(site_x, full_shape), jnp.broadcast_to(site_y, full_shape), jnp.broadcast_to(site_z, full_shape)]).astype(jnp.float32) + 0.5
    return lattice + jitter


def tile_lists(key):
    list_shape = (NBX // BX, NBY // BY, NBZ // BZ, TILES)
    block_x = jax.random.randint(jax.random.fold_in(key, 101), list_shape, 0, BX)
    block_y = jax.random.randint(jax.random.fold_in(key, 102), list_shape, 0, BY)
    block_z = jax.random.randint(jax.random.fold_in(key, 103), list_shape, 0, BZ)
    choose = jax.random.randint(jax.random.fold_in(key, 104), list_shape, 0, 27)
    shell = jnp.asarray(FULL_SHELL)
    slot = jnp.arange(TILES, dtype=jnp.int32)
    forced = slot < 6
    lower = slot % 2 == 0
    axis_id = slot // 2
    sign = jnp.where(lower, -1, 1).astype(jnp.int32)
    block_x = jnp.where(forced, jnp.where(lower, 0, BX - 1), block_x)
    block_y = jnp.where(forced, jnp.where(lower, 0, BY - 1), block_y)
    block_z = jnp.where(forced, jnp.where(lower, 0, BZ - 1), block_z)
    step_x = jnp.where(forced, sign * (axis_id == 0).astype(jnp.int32), jnp.take(shell[:, 0], choose))
    step_y = jnp.where(forced, sign * (axis_id == 1).astype(jnp.int32), jnp.take(shell[:, 1], choose))
    step_z = jnp.where(forced, sign * (axis_id == 2).astype(jnp.int32), jnp.take(shell[:, 2], choose))
    own_block = (block_x + 1) * ((BY + 2) * (BZ + 2)) + (block_y + 1) * (BZ + 2) + block_z + 1
    partner_block = own_block + step_x * ((BY + 2) * (BZ + 2)) + step_y * (BZ + 2) + step_z
    return (own_block.astype(jnp.int32), partner_block.astype(jnp.int32))


def draw_tile_own(key, part):
    return tile_lists(key)[0]


def draw_tile_partner(key, part):
    return tile_lists(key)[1]


def draw_tile_count(key, part):
    key = jax.random.fold_in(key, 21)
    grid_shape = (NBX // BX, NBY // BY, NBZ // BZ)
    lowered = jax.random.randint(jax.random.fold_in(key, 1), grid_shape, 0, 2)
    counts = TILES - TILES // 4 * lowered
    flat_counts = counts.reshape(-1)
    total = flat_counts.shape[0]
    chosen = jax.random.randint(jax.random.fold_in(key, 2), (), 0, total)
    other = (chosen + 1) % total
    flat_counts = flat_counts.at[chosen].set(TILES)
    flat_counts = flat_counts.at[other].set(TILES - TILES // 4)
    return flat_counts.reshape(grid_shape).astype(jnp.int32)


def draw_family_bits(key, part):
    key = jax.random.fold_in(key, 31)
    mask_shape = (NBX // BX, NBY // BY, NBZ // BZ, TILES, WORDS, BLK)
    first_word = jax.random.randint(jax.random.fold_in(key, 1), mask_shape, 0, 256)
    second_word = jax.random.randint(jax.random.fold_in(key, 2), mask_shape, 0, 256)
    packed = jnp.bitwise_or(first_word, second_word).astype(jnp.int32)
    return packed.at[0, 0, 0, 0, 0, 0].set(0)


def draw_broken_bits(key, part):
    key = jax.random.fold_in(key, 41)
    mask_shape = (NBX // BX, NBY // BY, NBZ // BZ, TILES, WORDS, BLK)
    first_word = jax.random.randint(jax.random.fold_in(key, 1), mask_shape, 0, 256)
    second_word = jax.random.randint(jax.random.fold_in(key, 2), mask_shape, 0, 256)
    third_word = jax.random.randint(jax.random.fold_in(key, 3), mask_shape, 0, 256)
    packed = jnp.bitwise_and(jnp.bitwise_and(first_word, second_word), third_word).astype(jnp.int32)
    return packed.at[0, 0, 0, 0, 0, 1].set(255)


def levels(key, shape, cuts, smallest, high):
    factor_of, own = 1.0, jax.random.fold_in(key, 6)
    for position, shards_of in cuts:
        draws = jnp.exp(jax.random.uniform(jax.random.fold_in(own, position), (shards_of,), jnp.float32, smallest / len(cuts), high / len(cuts)))
        factor_of = factor_of * jnp.repeat(draws, shape[position] // shards_of).reshape([-1 if axis == position else 1 for axis in range(len(shape))])
    return factor_of


def noise(own_key, dims, scale, reach, pieces=(), held_as=jnp.bfloat16):
    values = scale * jax.random.normal(own_key, dims, jnp.float32)
    if pieces:
        values = values * levels(own_key, dims, pieces, -0.22, 0.18)
    return jnp.clip(values, -reach, reach).astype(held_as)


def setup_inputs(seed: int = 0) -> dict:
    arg_keys = jax.random.split(jax.random.key(seed), 11)
    return {
        "positions": draw_positions(jax.random.fold_in(arg_keys[10], 71), 0),
        "volume": jnp.clip(jnp.exp(math.log(2.0) - 1.3862944 * jax.random.uniform(arg_keys[1], (NBX, NBY, NBZ, BLK), jnp.float32) ** levels(arg_keys[1], (NBX, NBY, NBZ, BLK), ((0, 8), (1, 8), (2, 8)), -0.2, 0.2)), 0.5, 2.0),
        "displacement": noise(arg_keys[2], (3, NBX, NBY, NBZ, BLK), 0.04, 0.12, ((1, 8), (2, 8), (3, 8)), jnp.float32),
        "velocity": noise(arg_keys[3], (3, NBX, NBY, NBZ, BLK), 0.25, 1.0, ((1, 8), (2, 8), (3, 8)), jnp.float32),
        "acceleration": noise(arg_keys[4], (3, NBX, NBY, NBZ, BLK), 1.0, 4.0, ((1, 8), (2, 8), (3, 8)), jnp.float32),
        "tile_own": draw_tile_own(jax.random.fold_in(arg_keys[10], 71), 0),
        "tile_partner": draw_tile_partner(jax.random.fold_in(arg_keys[10], 71), 0),
        "tile_count": draw_tile_count(jax.random.fold_in(arg_keys[10], 71), 0),
        "family_bits": draw_family_bits(jax.random.fold_in(arg_keys[10], 71), 0),
        "broken_bits": draw_broken_bits(jax.random.fold_in(arg_keys[10], 71), 0),
    }


K_BULK = 8000.0
MU_SHEAR = 600.0
VOLUME_FLOOR = 2000.0
TIME_DELTA = 0.05

def bond_bits(packed):
    by_rows = jnp.swapaxes(packed, 1, 2)
    spread = jnp.repeat(by_rows, 8, axis=2)
    bit_place = jnp.arange(spread.shape[2], dtype=jnp.int32) % 8
    return jnp.bitwise_and(jnp.right_shift(spread, bit_place), 1)

def bond_geometry(static_pad, disp_pad, own_block, partner_block, family, broken, live_slot):
    near_data = jnp.take(static_pad, own_block, axis=1)
    far_data = jnp.take(static_pad, partner_block, axis=1)
    near_disp = jnp.take(disp_pad, own_block, axis=1)
    far_disp = jnp.take(disp_pad, partner_block, axis=1)
    offset = far_data[:3, :, None, :] - near_data[:3, :, :, None]
    stretch = offset + far_disp[:, :, None, :] - near_disp[:, :, :, None]
    point_index = jnp.arange(offset.shape[3], dtype=jnp.int32)
    upper_half = point_index[None, :] > point_index[:, None]
    self_tile = (own_block == partner_block)[:, None, None]
    alive = bond_bits(family) * (1 - bond_bits(broken)) > 0
    alive = alive & (upper_half[None] | jnp.logical_not(self_tile)) & live_slot[:, None, None]
    weight = alive.astype(jnp.float32)
    rest_length = jnp.sqrt(jnp.where(alive, lax.optimization_barrier(jnp.sum(offset * offset, axis=0)), 1.0))
    bond_length = jnp.sqrt(jnp.where(alive, lax.optimization_barrier(jnp.sum(stretch * stretch, axis=0)), 1.0))
    return (weight, rest_length, bond_length - rest_length, stretch / bond_length, near_data[3], far_data[3])

def dilatation_terms(geometry, extra_data, own_block, partner_block):
    weight, rest_length, extension, unit_direction, near_volume, far_volume = geometry
    stretch_term = weight * rest_length * extension
    square = weight * rest_length * rest_length
    near_terms = jnp.stack([lax.optimization_barrier(jnp.sum(stretch_term * far_volume[:, None, :], axis=2)), lax.optimization_barrier(jnp.sum(square * far_volume[:, None, :], axis=2))])
    far_terms = jnp.stack([lax.optimization_barrier(jnp.sum(stretch_term * near_volume[:, :, None], axis=1)), lax.optimization_barrier(jnp.sum(square * near_volume[:, :, None], axis=1))])
    return (near_terms, far_terms)

def force_terms(geometry, coef_pad, own_block, partner_block):
    weight, rest_length, extension, unit_direction, near_volume, far_volume = geometry
    near_coef = jnp.take(coef_pad, own_block, axis=1)
    far_coef = jnp.take(coef_pad, partner_block, axis=1)
    magnitude = weight * (rest_length * (near_coef[0][:, :, None] + far_coef[0][:, None, :]) + extension * (near_coef[1][:, :, None] + far_coef[1][:, None, :]))
    bond_force = magnitude[None] * unit_direction
    near_terms = lax.optimization_barrier(jnp.sum(bond_force * far_volume[None, :, None, :], axis=3))
    far_terms = -lax.optimization_barrier(jnp.sum(bond_force * near_volume[None, :, :, None], axis=2))
    return (near_terms, far_terms)

def tile_pass(kernel, channels, static_pad, disp_pad, extra_data, own_list, partner_list, family, broken, live_count):
    running = jnp.zeros((channels, static_pad.shape[1], static_pad.shape[2]), jnp.float32)

    def group_step(group_index, running):
        first_slot = (group_index * GROUP).astype(jnp.int32)
        own_block = lax.dynamic_slice_in_dim(own_list, first_slot, GROUP)
        partner_block = lax.dynamic_slice_in_dim(partner_list, first_slot, GROUP)
        family_group = lax.dynamic_slice_in_dim(family, first_slot, GROUP)
        broken_group = lax.dynamic_slice_in_dim(broken, first_slot, GROUP)
        slot_index = first_slot + jnp.arange(GROUP, dtype=jnp.int32)
        geometry = bond_geometry(static_pad, disp_pad, own_block, partner_block, family_group, broken_group, slot_index < live_count)
        near_terms, far_terms = kernel(geometry, extra_data, own_block, partner_block)
        running = running.at[:, own_block].add(near_terms)
        return running.at[:, partner_block].add(far_terms)
    groups = ((live_count + GROUP - 1) // GROUP).astype(jnp.int32)
    return lax.fori_loop(jnp.int32(0), groups, group_step, running)

def material_coefs(volume_sums):
    floored = jnp.maximum(volume_sums[1], VOLUME_FLOOR)
    dilatation = 3.0 * volume_sums[0] / floored
    return jnp.stack([dilatation * (3.0 * K_BULK - 5.0 * MU_SHEAR) / floored, 15.0 * MU_SHEAR / floored])

def pad_blocks(values_in):
    return jnp.pad(values_in, ((0, 0), (1, 1), (1, 1), (1, 1), (0, 0)))

def flat_blocks(values_in):
    return values_in.reshape(values_in.shape[0], -1, values_in.shape[-1])

def window(values_in, corner, channels):
    return lax.dynamic_slice(values_in, corner, (channels, BX + 2, BY + 2, BZ + 2, BLK))

def global_pass(kernel, channels, static_all, disp_all, extra_all, extra_channels, tile_own, tile_partner, tile_count, family_bits, broken_bits):
    accumulated = jnp.zeros((channels, NBX + 2, NBY + 2, NBZ + 2, BLK), jnp.float32)

    def device_step(device, accumulated):
        device_id = jnp.asarray(device).astype(jnp.int32)
        index_x = device_id // (N_GY * N_GZ)
        index_y = device_id // N_GZ % N_GY
        index_z = device_id % N_GZ
        anchor = jnp.int32(0)
        corner = (anchor, (index_x * BX).astype(jnp.int32), (index_y * BY).astype(jnp.int32), (index_z * BZ).astype(jnp.int32), anchor)
        partial_value = tile_pass(kernel, channels, flat_blocks(window(static_all, corner, 4)), flat_blocks(window(disp_all, corner, 3)), flat_blocks(window(extra_all, corner, extra_channels)), tile_own[index_x, index_y, index_z], tile_partner[index_x, index_y, index_z], family_bits[index_x, index_y, index_z], broken_bits[index_x, index_y, index_z], tile_count[index_x, index_y, index_z])
        current = window(accumulated, corner, channels)
        return lax.dynamic_update_slice(accumulated, current + partial_value.reshape(current.shape), corner)
    accumulated = lax.fori_loop(0, N_GX * N_GY * N_GZ, device_step, accumulated)
    return accumulated[:, 1:-1, 1:-1, 1:-1]

def reference(positions, volume, displacement, velocity, acceleration, tile_own, tile_partner, tile_count, family_bits, broken_bits):
    static_all = pad_blocks(jnp.concatenate([positions, volume[None]], axis=0))
    for time_step in range(STEPS):
        half_vel = velocity + 0.5 * TIME_DELTA * acceleration
        displacement = displacement + TIME_DELTA * half_vel
        disp_all = pad_blocks(displacement)
        volume_sums = global_pass(dilatation_terms, 2, static_all, disp_all, static_all, 4, tile_own, tile_partner, tile_count, family_bits, broken_bits)
        coef_all = pad_blocks(material_coefs(volume_sums))
        acceleration = global_pass(force_terms, 3, static_all, disp_all, coef_all, 2, tile_own, tile_partner, tile_count, family_bits, broken_bits)
        velocity = half_vel + 0.5 * TIME_DELTA * acceleration
    return (displacement, velocity, acceleration)
```

```python
import functools

import jax
import jax.numpy as jnp
from jax import lax
from jax.experimental import pallas as pl
from jax.experimental.pallas import tpu as pltpu
from jax.sharding import PartitionSpec as P

BLK = 128
WORDS = 16
BX, BY, BZ = 4, 4, 2
TILES = 40
N_DEV = 8
K_BULK = 8000.0
MU_SHEAR = 600.0
VOLUME_FLOOR = 2000.0
TIME_DELTA = 0.05
TINY = 1e-30
UNROLL = 4
ROWS = (BY + 2) * (BZ + 2) * 8

YZ = [(-1, 0), (1, 0), (0, -1), (0, 1), (-1, -1), (-1, 1), (1, -1), (1, 1)]
OWN_ROWS = BY * BZ * 8
GHOST = dict(zip(YZ, (slice(64, 80), slice(80, 96), slice(96, 128), slice(128, 160), slice(160, 168), slice(168, 176), slice(176, 184), slice(184, 192))))
INNER = {
    (-1, 0): (0, 1),
    (1, 0): (6, 7),
    (0, -1): (0, 2, 4, 6),
    (0, 1): (1, 3, 5, 7),
    (-1, -1): (0,),
    (-1, 1): (1,),
    (1, -1): (6,),
    (1, 1): (7,),
}


def slot(step):
    rows = GHOST[step]
    return slice(rows.start - OWN_ROWS, rows.stop - OWN_ROWS)


def column(g):
    return slice(g * 8, g * 8 + 8)


def plane(x):
    return pl.ds(x, 8, stride=8)


def kernel(
    pos,
    vol,
    dis,
    vel,
    acc,
    own,
    par,
    cnt,
    fam_hbm,
    brk_hbm,
    out_u,
    out_v,
    out_a,
    fam,
    brk,
    near_at,
    far_at,
    data,
    xrel,
    ypos,
    half,
    base,
    inv,
    kap,
    w_ref,
    r_ref,
    e_ref,
    n_ref,
    col_x,
    col_y,
    col_c,
    hot_t,
    hot,
    terms,
    sum_s1,
    sum_f1,
    sum_s2,
    sum_f2,
    coef1,
    coef2,
    disp2,
    fold_s1,
    fold_f1,
    fold_s2,
    fold_f2,
    zs0,
    zs1,
    zs2,
    zs3,
    xs0,
    xr0,
    xsb,
    xrb,
    xs1,
    xr1,
    xs2,
    xr2,
    xs3,
    xr3,
    xs4,
    xr4,
    send_sem,
    recv_sem,
    load_sem,
):
    gx, gy, gz = lax.axis_index("gx"), lax.axis_index("gy"), lax.axis_index("gz")
    sent = []
    counter = [0]

    def there(step):
        ok = None
        for at, d in zip((gx, gy, gz), step):
            if d:
                test = at > 0 if d < 0 else at < N_DEV - 1
                ok = test if ok is None else jnp.logical_and(ok, test)
        return ok

    def target(step):
        return tuple(at + d for at, d in zip((gx, gy, gz), step))

    class Exchange:
        def __init__(self, steps, source, sink):
            self.steps, self.base = steps, counter[0]
            counter[0] += len(steps)
            self.source, self.sink = source, sink
            sent.append(self)

        def copy(self, i, step, back):
            opposite = tuple(-d for d in step)
            return pltpu.make_async_remote_copy(
                src_ref=self.source(step),
                dst_ref=self.sink(step if back else opposite),
                send_sem=send_sem.at[self.base + i],
                recv_sem=recv_sem.at[self.base + (i if back else self.steps.index(opposite))],
                device_id=target(step),
                device_id_type=pl.DeviceIdType.MESH,
            )

        def start(self):
            for i, step in enumerate(self.steps):
                pl.when(there(step))(lambda i=i, step=step: self.copy(i, step, False).start())

        def arrive(self):
            for i, step in enumerate(self.steps):
                pl.when(there(step))(lambda i=i, step=step: self.copy(i, step, True).wait_recv())

        def finish(self):
            for i, step in enumerate(self.steps):
                pl.when(there(step))(lambda i=i, step=step: self.copy(i, step, False).wait_send())

    yz_steps = [(0, dy, dz) for dy, dz in YZ]
    x_steps = [(-1, 0, 0), (1, 0, 0)]

    def fold_exchange(sums, fold):
        return Exchange(
            yz_steps,
            lambda s: sums.at[:, GHOST[s[1:]]],
            lambda s: fold.at[:, slot(s[1:])],
        )

    def add_folds(sums, fold, channels):
        for c in range(channels):
            for g in range(BY * BZ):
                total = sums[c, column(g)]
                for step in YZ:
                    if g in INNER[step]:
                        first = slot(step).start + INNER[step].index(g) * 8
                        total = total + fold[c, first : first + 8]
                sums[c, column(g)] = total

    def halo_exchange(array, packed, channels):
        def source(s):
            step = s[1:]
            if step[0] == 0:
                return packed.at[(step[1] + 1) // 2]
            groups = INNER[step]
            return array.at[:, groups[0] * 8 : groups[-1] * 8 + 8]

        for side in (0, 1):
            for j in range(BY):
                for c in range(channels):
                    packed[side, c, column(j)] = array[c, column(2 * j + side)]
        return Exchange(yz_steps, source, lambda s: array.at[:, GHOST[s[1:]]])

    def x_exchange(send, recv):
        return Exchange(
            x_steps, lambda s: send.at[(s[0] + 1) // 2], lambda s: recv.at[(s[0] + 1) // 2]
        )

    def shared(side):
        return ((0, 1), (BX, BX + 1))[side]

    def pack_x(send, array, channels):
        for side in (0, 1):
            for c in range(channels):
                for j, x in enumerate(shared(side)):
                    send[side, c, column(j)] = array[c, plane(x), :]

    def add_x(array, recv, channels):
        for side in (0, 1):
            for c in range(channels):
                for j, x in enumerate(shared(side)):
                    array[c, plane(x), :] = array[c, plane(x), :] + recv[side, c, column(j)]

    barrier = pltpu.get_barrier_semaphore()
    expected = jnp.int32(0)
    for step in x_steps + yz_steps:
        expected = expected + there(step).astype(jnp.int32)

        @pl.when(there(step))
        def _(step=step):
            pl.semaphore_signal(
                barrier, inc=1, device_id=target(step), device_id_type=pl.DeviceIdType.MESH
            )

    load_f = pltpu.make_async_copy(fam_hbm, fam, load_sem.at[0])
    load_b = pltpu.make_async_copy(brk_hbm, brk, load_sem.at[1])
    load_f.start()
    load_b.start()

    for x in range(BX):
        data[3, plane(x + 1), :] = vol[x]
        for k in range(3):
            data[k, plane(x + 1), :] = pos[k, x]
            h = vel[k, x] + 0.5 * TIME_DELTA * acc[k, x]
            u1 = dis[k, x] + TIME_DELTA * h
            data[4 + k, plane(x + 1), :] = u1
            half[k, x] = h
            base[k, plane(x + 1), :] = u1 + TIME_DELTA * h
    for side, x in ((0, 1), (1, BX)):
        for c in range(7):
            xs0[side, c] = data[c, plane(x), :]
        for c in range(3):
            xsb[side, c] = base[c, plane(x), :]

    pl.semaphore_wait(barrier, expected)
    x0 = x_exchange(xs0, xr0)
    xb = x_exchange(xsb, xrb)
    x0.start()

    for side, step in enumerate(x_steps):

        @pl.when(jnp.logical_not(there(step)))
        def _(side=side):
            for ref in (xr0, xrb, xr1, xr2, xr3, xr4):
                ref[side] = jnp.zeros(ref.shape[1:], jnp.float32)

    for step in YZ:

        @pl.when(jnp.logical_not(there((0,) + step)))
        def _(step=step):
            for ref in (data, coef1, disp2, coef2):
                rows = GHOST[step]
                ref[:, rows] = jnp.zeros((ref.shape[0], rows.stop - rows.start, BLK), jnp.float32)
            for ref in (fold_s1, fold_f1, fold_s2, fold_f2):
                rows = slot(step)
                ref[:, rows] = jnp.zeros((ref.shape[0], rows.stop - rows.start, BLK), jnp.float32)

    terms[...] = jnp.zeros_like(terms)
    hot_t[...] = jnp.zeros_like(hot_t)
    org = [g.astype(jnp.float32) * 16.0 for g in (gx, gy, gz)]
    load_f.wait()
    load_b.wait()
    sub = lax.broadcasted_iota(jnp.int32, (BLK, BLK), 0)
    lane = lax.broadcasted_iota(jnp.int32, (BLK, BLK), 1)

    def row_of(block):
        x, g = block // 24, block % 24
        y, z = g // 4, g % 4
        inside_y, inside_z = (y >= 1) & (y <= BY), (z >= 1) & (z <= BZ)
        upper_y, upper_z = (y > BY).astype(jnp.int32), (z > BZ).astype(jnp.int32)
        at_y = jnp.where(inside_z, 8 + 2 * upper_y + z - 1, 20 + 2 * upper_y + upper_z)
        in_y = jnp.where(inside_z, (y - 1) * 2 + z - 1, 12 + 4 * upper_z + y - 1)
        return jnp.where(inside_y, in_y, at_y) * 8 + x

    def mask_body(t, carry):
        a, b = own[t], par[t]
        row_a, row_b = row_of(a), row_of(b)
        near_at[t] = jnp.clip(row_a // 8 * BX + row_a % 8 - 1, 0, BX * BY * BZ - 1)
        far_at[t] = jnp.clip(row_b, 0, ROWS - 1)
        apart = (a != b).astype(jnp.int32)
        live = (t < cnt[0, 0, 0]).astype(jnp.int32)
        shift = lax.broadcasted_iota(jnp.int32, (8, BLK), 0)
        rows = []
        for g in range(WORDS):
            word = fam[t, pl.ds(g, 1), :] & ~brk[t, pl.ds(g, 1), :]
            rows.append((jnp.broadcast_to(word, (8, BLK)) >> shift) & 1)
        bits = jnp.concatenate(rows, axis=0)
        bits = bits & ((sub > lane).astype(jnp.int32) | apart) & live
        w_ref[t] = bits.astype(jnp.float32).T
        code = lax.broadcasted_iota(jnp.int32, (1, BLK), 1)
        for half_at in range(2):
            hot_t[half_at, pl.ds(2 * t, 1), :] = (code + 128 * half_at == row_a).astype(jnp.float32)
            hot_t[half_at, pl.ds(2 * t + 1, 1), :] = (code + 128 * half_at == row_b).astype(
                jnp.float32
            )
        return carry

    lax.fori_loop(0, TILES, mask_body, 0, unroll=UNROLL)
    picked = jnp.concatenate([hot_t[0].T, hot_t[1].T], axis=0)[0:ROWS].astype(jnp.bfloat16)
    hot[:, 0:128] = picked
    hot[:, 128:256] = picked

    def put_columns(dest, first, values):
        def body(g, carry):
            rows = pl.ds(pl.multiple_of(g * 8, 8), 8)
            for k, value in enumerate(values(rows)):
                turned = value.T
                for x in range(BX):
                    dest[g * BX + x, first + k] = jnp.broadcast_to(
                        turned[:, x + 1 : x + 2], (BLK, BLK)
                    )
            return carry

        lax.fori_loop(0, BY * BZ, body, 0)

    put_columns(
        col_x, 0, lambda rows: [data[k, rows, :] - org[k] for k in range(3)] + [data[3, rows, :]]
    )
    put_columns(
        col_y,
        0,
        lambda rows: [(data[k, rows, :] - org[k]) + data[4 + k, rows, :] for k in range(3)],
    )

    x0.arrive()
    for side, x in ((0, 0), (1, BX + 1)):
        for c in range(7):
            data[c, plane(x), :] = xr0[side, c]
    h0 = halo_exchange(data, zs0, 7)
    h0.start()
    xb.start()
    volume = data[3, 0:OWN_ROWS]
    inv[...] = jnp.where(volume > 0.0, 1.0 / jnp.where(volume > 0.0, volume, 1.0), 0.0)
    h0.arrive()
    for k in range(3):
        xrel[k] = data[k] - org[k]
        ypos[k] = xrel[k] + data[4 + k]

    def far_row(ref, k, at):
        return ref[k, pl.ds(at, 1), :]

    diagonal = sub == lane

    def put_sums(t, c, values, far_sign=1):
        per_a = jnp.sum(values, axis=1, keepdims=True)
        near = jnp.sum(jnp.where(diagonal, per_a, 0.0), axis=0, keepdims=True)
        far = jnp.sum(values, axis=0, keepdims=True)
        terms[c, pl.ds(2 * t, 1), :] = near
        terms[c, pl.ds(2 * t + 1, 1), :] = far if far_sign > 0 else -far

    def gather_sums(sums, channels):
        full = jnp.concatenate([terms[c] for c in range(channels)], axis=1)
        high = full.astype(jnp.bfloat16)
        low = (full - high.astype(jnp.float32)).astype(jnp.bfloat16)
        out = jnp.dot(
            hot[...], jnp.concatenate([high, low], axis=0), preferred_element_type=jnp.float32
        )
        for c in range(channels):
            sums[c] = out[:, c * 128 : (c + 1) * 128]

    def deformed(near, at):
        d = [far_row(ypos, k, at) - col_y[near, k] for k in range(3)]
        square = jnp.maximum(d[0] * d[0] + d[1] * d[1] + d[2] * d[2], TINY)
        inverse = lax.rsqrt(square)
        return d, square * inverse, inverse

    def first_body(t, carry):
        near, at = near_at[t], far_at[t]
        o = [far_row(xrel, k, at) - col_x[near, k] for k in range(3)]
        square = jnp.maximum(o[0] * o[0] + o[1] * o[1] + o[2] * o[2], TINY)
        rest = square * lax.rsqrt(square)
        weight = w_ref[t] * (col_x[near, 3] * far_row(data, 3, at))
        w_ref[t] = weight
        r_ref[t] = rest
        weighted = weight * rest
        put_sums(t, 1, weighted * rest)
        _, length, _ = deformed(near, at)
        put_sums(t, 0, weighted * (length - rest))
        return carry

    def sum_body(t, carry):
        near, at = near_at[t], far_at[t]
        _, length, _ = deformed(near, at)
        rest = r_ref[t]
        put_sums(t, 0, w_ref[t] * rest * (length - rest))
        return carry

    def geometry_body(t, carry):
        near, at = near_at[t], far_at[t]
        d, length, inverse = deformed(near, at)
        e_ref[t] = length - r_ref[t]
        scale = w_ref[t] * inverse
        for k in range(3):
            n_ref[t, k] = scale * d[k]
        return carry

    def force_body(far_p, t, carry):
        near, at = near_at[t], far_at[t]
        c = r_ref[t] * (col_c[near, 0] + far_row(far_p, 0, at))
        c = c + e_ref[t] * (col_c[near, 1] + far_row(coef1, 1, at))
        for k in range(3):
            put_sums(t, k, c * n_ref[t, k], far_sign=-1)
        return carry

    def tiles(body):
        lax.fori_loop(0, TILES, body, 0, unroll=UNROLL)

    own_rows = slice(0, OWN_ROWS)

    tiles(first_body)
    gather_sums(sum_s1, 2)
    f = fold_exchange(sum_s1, fold_s1)
    f.start()
    f.arrive()
    add_folds(sum_s1, fold_s1, 2)
    pack_x(xs1, sum_s1, 2)
    x1 = x_exchange(xs1, xr1)
    x1.start()
    tiles(geometry_body)
    x1.arrive()
    add_x(sum_s1, xr1, 2)
    floored = jnp.maximum(sum_s1[1, own_rows] * inv[...], VOLUME_FLOOR)
    kap[...] = (3.0 * (3.0 * K_BULK - 5.0 * MU_SHEAR)) * inv[...] / floored / floored
    coef1[0, own_rows] = sum_s1[0, own_rows] * kap[...]
    coef1[1, own_rows] = 15.0 * MU_SHEAR / floored
    h1 = halo_exchange(coef1, zs1, 2)
    h1.start()
    put_columns(col_c, 0, lambda rows: [coef1[k, rows, :] for k in range(2)])
    h1.arrive()

    tiles(functools.partial(force_body, coef1))
    gather_sums(sum_f1, 3)
    f = fold_exchange(sum_f1, fold_f1)
    f.start()
    xb.arrive()
    for side, x in ((0, 0), (1, BX + 1)):
        for k in range(3):
            base[k, plane(x), :] = xrb[side, k]
    f.arrive()
    add_folds(sum_f1, fold_f1, 3)
    pack_x(xs2, sum_f1, 3)
    x2 = x_exchange(xs2, xr2)
    x2.start()
    x2.arrive()
    add_x(sum_f1, xr2, 3)
    for k in range(3):
        force = sum_f1[k, own_rows] * inv[...]
        sum_f1[k, own_rows] = force
        disp2[k, own_rows] = base[k] + (TIME_DELTA * TIME_DELTA) * force
    h2 = halo_exchange(disp2, zs2, 3)
    h2.start()
    put_columns(
        col_y, 0, lambda rows: [xrel[k, rows, :] + disp2[k, rows, :] for k in range(3)]
    )
    for x in range(BX):
        for k in range(3):
            half[k, x] = half[k, x] + TIME_DELTA * sum_f1[k, plane(x + 1), :]
    h2.arrive()
    for k in range(3):
        ypos[k] = xrel[k] + disp2[k]

    tiles(sum_body)
    gather_sums(sum_s2, 1)
    f = fold_exchange(sum_s2, fold_s2)
    f.start()
    f.arrive()
    add_folds(sum_s2, fold_s2, 1)
    pack_x(xs3, sum_s2, 1)
    x3 = x_exchange(xs3, xr3)
    x3.start()
    tiles(geometry_body)
    x3.arrive()
    add_x(sum_s2, xr3, 1)
    coef2[0, own_rows] = sum_s2[0, own_rows] * kap[...]
    h3 = halo_exchange(coef2, zs3, 1)
    h3.start()
    put_columns(col_c, 0, lambda rows: [coef2[0, rows, :]])
    h3.arrive()

    tiles(functools.partial(force_body, coef2))
    gather_sums(sum_f2, 3)
    f = fold_exchange(sum_f2, fold_f2)
    f.start()
    f.arrive()
    add_folds(sum_f2, fold_f2, 3)
    for side, x in ((0, 0), (1, BX + 1)):
        for k in range(3):
            xs4[side, k] = sum_f2[k, plane(x), :]
    x4 = x_exchange(xs4, xr4)
    x4.start()
    for x in range(BX):
        for k in range(3):
            out_u[k, x] = disp2[k, plane(x + 1), :]
    x4.arrive()
    for x in range(BX):
        for k in range(3):
            force = sum_f2[k, plane(x + 1), :]
            if x == 0:
                force = force + xr4[0, k]
            if x == BX - 1:
                force = force + xr4[1, k]
            force = force * inv[plane(x + 1), :]
            out_a[k, x] = force
            out_v[k, x] = half[k, x] + 0.5 * TIME_DELTA * force
    for exchange in sent:
        exchange.finish()


def per_device(
    positions,
    volume,
    displacement,
    velocity,
    acceleration,
    tile_own,
    tile_partner,
    tile_count,
    family_bits,
    broken_bits,
):
    vmem = pl.BlockSpec(memory_space=pltpu.VMEM)
    smem = pl.BlockSpec(memory_space=pltpu.SMEM)
    hbm = pl.BlockSpec(memory_space=pl.ANY)
    out = jax.ShapeDtypeStruct((3, BX, BY * BZ, BLK), jnp.float32)

    def buf(*shape, dtype=jnp.float32):
        return pltpu.VMEM(shape, dtype)

    def grid(channels):
        return buf(channels, ROWS, BLK)

    def fold(channels):
        return buf(channels, ROWS - OWN_ROWS, BLK)

    def pair(channels, rows):
        return [buf(2, channels, rows, BLK), buf(2, channels, rows, BLK)]

    bits = pltpu.VMEM((TILES, WORDS, BLK), jnp.int32)
    copies = 8 * len(YZ) + 6 * 2
    values = (positions, displacement, velocity, acceleration)
    pos, dis, vel, acc = (v.reshape(3, BX, BY * BZ, BLK) for v in values)
    outs = pl.pallas_call(
        kernel,
        out_shape=[out] * 3,
        in_specs=[vmem] * 5 + [smem] * 3 + [hbm] * 2,
        out_specs=[vmem] * 3,
        scratch_shapes=[
            bits,
            bits,
            pltpu.SMEM((TILES,), jnp.int32),
            pltpu.SMEM((TILES,), jnp.int32),
            grid(7),
            grid(3),
            grid(3),
            buf(3, BX, BY * BZ, BLK),
            buf(3, OWN_ROWS, BLK),
            buf(OWN_ROWS, BLK),
            buf(OWN_ROWS, BLK),
            buf(TILES, BLK, BLK),
            buf(TILES, BLK, BLK),
            buf(TILES, BLK, BLK),
            buf(TILES, 3, BLK, BLK),
            buf(BX * BY * BZ, 4, BLK, BLK),
            buf(BX * BY * BZ, 3, BLK, BLK),
            buf(BX * BY * BZ, 2, BLK, BLK),
            buf(2, 128, 128),
            buf(ROWS, 256, dtype=jnp.bfloat16),
            buf(3, 128, 128),
            grid(2),
            grid(3),
            grid(1),
            grid(3),
            grid(2),
            grid(1),
            grid(3),
            fold(2),
            fold(3),
            fold(1),
            fold(3),
            buf(2, 7, BY * 8, BLK),
            buf(2, 2, BY * 8, BLK),
            buf(2, 3, BY * 8, BLK),
            buf(2, 1, BY * 8, BLK),
            *pair(7, 8),
            *pair(3, 8),
            *pair(2, 16),
            *pair(3, 16),
            *pair(1, 16),
            *pair(3, 8),
            pltpu.SemaphoreType.DMA((copies,)),
            pltpu.SemaphoreType.DMA((copies,)),
            pltpu.SemaphoreType.DMA((2,)),
        ],
        compiler_params=pltpu.CompilerParams(
            collective_id=0, has_side_effects=True, vmem_limit_bytes=56 * 1024 * 1024
        ),
    )(
        pos,
        volume.reshape(BX, BY * BZ, BLK),
        dis,
        vel,
        acc,
        tile_own.reshape(TILES),
        tile_partner.reshape(TILES),
        tile_count,
        family_bits.reshape(TILES, WORDS, BLK),
        broken_bits.reshape(TILES, WORDS, BLK),
    )
    return tuple(v.reshape(3, BX, BY, BZ, BLK) for v in outs)


def solution(mesh):
    in_specs = (
        P(None, "gx", "gy", "gz", None),
        P("gx", "gy", "gz", None),
        P(None, "gx", "gy", "gz", None),
        P(None, "gx", "gy", "gz", None),
        P(None, "gx", "gy", "gz", None),
        P("gx", "gy", "gz", None),
        P("gx", "gy", "gz", None),
        P("gx", "gy", "gz"),
        P("gx", "gy", "gz", None, None, None),
        P("gx", "gy", "gz", None, None, None),
    )
    out_specs = (
        P(None, "gx", "gy", "gz", None),
        P(None, "gx", "gy", "gz", None),
        P(None, "gx", "gy", "gz", None),
    )
    return jax.shard_map(
        per_device, mesh=mesh, in_specs=in_specs, out_specs=out_specs, check_vma=False
    )
```

```python
import functools

import jax
import jax.numpy as jnp
from jax import lax
from jax.experimental import pallas as pl
from jax.experimental.pallas import tpu as pltpu
from jax.sharding import PartitionSpec as P

BLK = 128
WORDS = 16
BX, BY, BZ = 4, 4, 2
TILES = 40
N_DEV = 8
K_BULK = 8000.0
MU_SHEAR = 600.0
VOLUME_FLOOR = 2000.0
TIME_DELTA = 0.05
TINY = 1e-30
UNROLL = 8
ROWS = (BY + 2) * (BZ + 2) * 8

YZ = [(-1, 0), (1, 0), (0, -1), (0, 1), (-1, -1), (-1, 1), (1, -1), (1, 1)]
OWN_ROWS = BY * BZ * 8
GHOST = dict(zip(YZ, (slice(64, 80), slice(80, 96), slice(96, 128), slice(128, 160), slice(160, 168), slice(168, 176), slice(176, 184), slice(184, 192))))
INNER = {
    (-1, 0): (0, 1),
    (1, 0): (6, 7),
    (0, -1): (0, 2, 4, 6),
    (0, 1): (1, 3, 5, 7),
    (-1, -1): (0,),
    (-1, 1): (1,),
    (1, -1): (6,),
    (1, 1): (7,),
}


def slot(step):
    rows = GHOST[step]
    return slice(rows.start - OWN_ROWS, rows.stop - OWN_ROWS)


def column(g):
    return slice(g * 8, g * 8 + 8)


def plane(x):
    return pl.ds(x, 8, stride=8)


def kernel(
    pos,
    vol,
    dis,
    vel,
    acc,
    own,
    par,
    cnt,
    fam_hbm,
    brk_hbm,
    out_u,
    out_v,
    out_a,
    fam,
    brk,
    near_at,
    far_at,
    data,
    xrel,
    ypos,
    half,
    base,
    inv,
    w_ref,
    r_ref,
    e_ref,
    n_ref,
    col_x,
    col_y,
    col_c,
    hot_t,
    hot,
    terms,
    sum_m,
    sum_s1,
    sum_f1,
    sum_s2,
    sum_f2,
    tot1,
    tot2,
    kapq,
    coef1,
    coef2,
    disp2,
    fold_m,
    fold_s1,
    fold_f1,
    fold_s2,
    fold_f2,
    zs0,
    zsm,
    zs1,
    zs2,
    zs3,
    xs0,
    xr0,
    xsb,
    xrb,
    xsm,
    xrm,
    xs1,
    xr1,
    xs2,
    xr2,
    xs3,
    xr3,
    xs4,
    xr4,
    zf1,
    yf1,
    cf1,
    zg1,
    yg1,
    cg1,
    zf2,
    yf2,
    cf2,
    zg2,
    yg2,
    cg2,
    send_sem,
    recv_sem,
    load_sem,
):
    gx, gy, gz = lax.axis_index("gx"), lax.axis_index("gy"), lax.axis_index("gz")
    counter = [0]
    pending = []

    def there(step):
        ok = None
        for at, d in zip((gx, gy, gz), step):
            if d:
                test = at > 0 if d < 0 else at < N_DEV - 1
                ok = test if ok is None else jnp.logical_and(ok, test)
        return ok

    def target(step):
        return tuple(at + d for at, d in zip((gx, gy, gz), step))

    class Exchange:
        def __init__(self, steps, source, sink):
            self.steps, self.base = steps, counter[0]
            counter[0] += len(steps)
            self.source, self.sink = source, sink
            pending.append(self)

        def copy(self, i, step, back):
            opposite = tuple(-d for d in step)
            return pltpu.make_async_remote_copy(
                src_ref=self.source(step),
                dst_ref=self.sink(step if back else opposite),
                send_sem=send_sem.at[self.base + i],
                recv_sem=recv_sem.at[self.base + (i if back else self.steps.index(opposite))],
                device_id=target(step),
                device_id_type=pl.DeviceIdType.MESH,
            )

        def start(self):
            for i, step in enumerate(self.steps):
                pl.when(there(step))(lambda i=i, step=step: self.copy(i, step, False).start())

        def arrive(self):
            for i, step in enumerate(self.steps):
                pl.when(there(step))(lambda i=i, step=step: self.copy(i, step, True).wait_recv())

        def finish(self):
            for i, step in enumerate(self.steps):
                pl.when(there(step))(lambda i=i, step=step: self.copy(i, step, False).wait_send())

    def settle():
        while pending:
            pending.pop(0).finish()

    yz_steps = [(0, dy, dz) for dy, dz in YZ]
    diagonal_steps = [(dx, dy, dz) for dx in (-1, 1) for dy, dz in YZ]
    x_steps = [(-1, 0, 0), (1, 0, 0)]

    def fold_exchange(sums, fold):
        return Exchange(
            yz_steps,
            lambda s: sums.at[:, GHOST[s[1:]]],
            lambda s: fold.at[:, slot(s[1:])],
        )

    def add_folds(dest, sums, fold, channels):
        for c in range(channels):
            for g in range(BY * BZ):
                total = sums[c, column(g)]
                for step in YZ:
                    if g in INNER[step]:
                        first = slot(step).start + INNER[step].index(g) * 8
                        total = total + fold[c, first : first + 8]
                dest[c, column(g)] = total

    def halo_exchange(array, packed, first, last):
        def source(s):
            step = s[1:]
            if step[0] == 0:
                return packed.at[(step[1] + 1) // 2, first:last]
            groups = INNER[step]
            return array.at[first:last, groups[0] * 8 : groups[-1] * 8 + 8]

        for side in (0, 1):
            for j in range(BY):
                for c in range(first, last):
                    packed[side, c, column(j)] = array[c, column(2 * j + side)]
        return Exchange(yz_steps, source, lambda s: array.at[first:last, GHOST[s[1:]]])

    def x_exchange(send, recv, first, last):
        return Exchange(
            x_steps,
            lambda s: send.at[(s[0] + 1) // 2, first:last],
            lambda s: recv.at[(s[0] + 1) // 2, first:last],
        )

    def diagonal_exchange(send, recv):
        def of(buffers, s):
            faces_z, faces_y, corners = buffers
            x, y, z = ((d + 1) // 2 for d in s)
            if s[1] == 0:
                return faces_z.at[x, z]
            return faces_y.at[x, y] if s[2] == 0 else corners.at[x, 2 * y + z]

        return Exchange(diagonal_steps, lambda s: of(send, s), lambda s: of(recv, s))

    def pack_diagonal(send, array):
        faces_z, faces_y, corners = send
        for side in (0, 1):
            for j, x in enumerate(shared(side)):
                for i in (0, 1):
                    faces_z[side, i, j * 4 : j * 4 + 4] = array[0, pl.ds(8 * i + x, 4, stride=16), :]
                    faces_y[side, i, j * 2 : j * 2 + 2] = array[0, pl.ds(48 * i + x, 2, stride=8), :]
                for i, g in enumerate((0, 1, 6, 7)):
                    corners[side, i, j : j + 1] = array[0, pl.ds(g * 8 + x, 1), :]

    def add_diagonal(array, recv):
        faces_z, faces_y, corners = recv
        for side in (0, 1):
            for j, x in enumerate(shared(side)):
                for i, d in enumerate((-1, 1)):
                    at = pl.ds(GHOST[(0, d)].start + x, 4, stride=8)
                    array[0, at, :] = array[0, at, :] + faces_z[side, i, j * 4 : j * 4 + 4]
                    at = pl.ds(GHOST[(d, 0)].start + x, 2, stride=8)
                    array[0, at, :] = array[0, at, :] + faces_y[side, i, j * 2 : j * 2 + 2]
                for i in range(4):
                    at = pl.ds(GHOST[(i // 2 * 2 - 1, i % 2 * 2 - 1)].start + x, 1)
                    array[0, at, :] = array[0, at, :] + corners[side, i, j : j + 1]

    def shared(side):
        return ((0, 1), (BX, BX + 1))[side]

    def pack_x(send, array, channels):
        for side in (0, 1):
            for c in range(channels):
                for j, x in enumerate(shared(side)):
                    send[side, c, column(j)] = array[c, plane(x), :]

    def add_x(array, recv, channels):
        for side in (0, 1):
            for c in range(channels):
                for j, x in enumerate(shared(side)):
                    array[c, plane(x), :] = array[c, plane(x), :] + recv[side, c, column(j)]

    barrier = pltpu.get_barrier_semaphore()
    expected = jnp.int32(0)
    for step in x_steps + yz_steps + diagonal_steps:
        expected = expected + there(step).astype(jnp.int32)

        @pl.when(there(step))
        def _(step=step):
            pl.semaphore_signal(
                barrier, inc=1, device_id=target(step), device_id_type=pl.DeviceIdType.MESH
            )

    load_f = pltpu.make_async_copy(fam_hbm, fam, load_sem.at[0])
    load_b = pltpu.make_async_copy(brk_hbm, brk, load_sem.at[1])
    load_f.start()
    load_b.start()

    for x in range(BX):
        data[3, plane(x + 1), :] = vol[x]
        for k in range(3):
            data[k, plane(x + 1), :] = pos[k, x]
    for side, x in ((0, 0), (1, BX - 1)):
        xs0[side, 3] = vol[x]
        for k in range(3):
            xs0[side, k] = pos[k, x]
    pl.semaphore_wait(barrier, expected)
    xv = x_exchange(xs0, xr0, 0, 4)
    xv.start()
    for x in (0, BX - 1, 1, 2):
        for k in range(3):
            h = vel[k, x] + 0.5 * TIME_DELTA * acc[k, x]
            u1 = dis[k, x] + TIME_DELTA * h
            data[4 + k, plane(x + 1), :] = u1
            half[k, x] = h
            base[k, plane(x + 1), :] = u1 + TIME_DELTA * h
            if x == 0 or x == BX - 1:
                xs0[x // (BX - 1), 4 + k] = u1
                xsb[x // (BX - 1), k] = u1 + TIME_DELTA * h
    xu = x_exchange(xs0, xr0, 4, 7)
    xb = x_exchange(xsb, xrb, 0, 3)
    xu.start()

    for side, step in enumerate(x_steps):

        @pl.when(jnp.logical_not(there(step)))
        def _(side=side):
            for ref in (xr0, xrb, xrm, xr1, xr2, xr3, xr4):
                ref[side] = jnp.zeros(ref.shape[1:], jnp.float32)

    for step in diagonal_steps:

        @pl.when(jnp.logical_not(there(step)))
        def _(step=step):
            x, y, z = ((d + 1) // 2 for d in step)
            for faces_z, faces_y, corners in ((zg1, yg1, cg1), (zg2, yg2, cg2)):
                if step[1] == 0:
                    faces_z[x, z] = jnp.zeros((8, BLK), jnp.float32)
                elif step[2] == 0:
                    faces_y[x, y] = jnp.zeros((4, BLK), jnp.float32)
                else:
                    corners[x, 2 * y + z] = jnp.zeros((2, BLK), jnp.float32)

    for step in YZ:

        @pl.when(jnp.logical_not(there((0,) + step)))
        def _(step=step):
            for ref in (data, kapq, disp2, tot1, tot2):
                rows = GHOST[step]
                ref[:, rows] = jnp.zeros((ref.shape[0], rows.stop - rows.start, BLK), jnp.float32)
            for ref in (fold_m, fold_s1, fold_f1, fold_s2, fold_f2):
                rows = slot(step)
                ref[:, rows] = jnp.zeros((ref.shape[0], rows.stop - rows.start, BLK), jnp.float32)

    hot_t[...] = jnp.zeros_like(hot_t)
    org = [g.astype(jnp.float32) * 16.0 for g in (gx, gy, gz)]
    load_f.wait()
    load_b.wait()
    sub = lax.broadcasted_iota(jnp.int32, (BLK, BLK), 0)
    lane = lax.broadcasted_iota(jnp.int32, (BLK, BLK), 1)

    def row_of(block):
        x, g = block // 24, block % 24
        y, z = g // 4, g % 4
        inside_y, inside_z = (y >= 1) & (y <= BY), (z >= 1) & (z <= BZ)
        upper_y, upper_z = (y > BY).astype(jnp.int32), (z > BZ).astype(jnp.int32)
        at_y = jnp.where(inside_z, 8 + 2 * upper_y + z - 1, 20 + 2 * upper_y + upper_z)
        in_y = jnp.where(inside_z, (y - 1) * 2 + z - 1, 12 + 4 * upper_z + y - 1)
        return jnp.where(inside_y, in_y, at_y) * 8 + x

    def mask_body(t, carry):
        a, b = own[t], par[t]
        row_a, row_b = row_of(a), row_of(b)
        near_at[t] = jnp.clip(row_a // 8 * BX + row_a % 8 - 1, 0, BX * BY * BZ - 1)
        far_at[t] = jnp.clip(row_b, 0, ROWS - 1)
        apart = (a != b).astype(jnp.int32)
        live = (t < cnt[0, 0, 0]).astype(jnp.int32)
        shift = lax.broadcasted_iota(jnp.int32, (8, BLK), 0)
        rows = []
        for g in range(WORDS):
            word = fam[t, pl.ds(g, 1), :] & ~brk[t, pl.ds(g, 1), :]
            rows.append((jnp.broadcast_to(word, (8, BLK)) >> shift) & 1)
        bits = jnp.concatenate(rows, axis=0)
        bits = bits & ((sub > lane).astype(jnp.int32) | apart) & live
        w_ref[t] = bits.astype(jnp.float32).T
        code = lax.broadcasted_iota(jnp.int32, (1, BLK), 1)
        for half_at in range(2):
            hot_t[half_at, pl.ds(2 * t, 1), :] = (code + 128 * half_at == row_a).astype(jnp.float32)
            hot_t[half_at, pl.ds(2 * t + 1, 1), :] = (code + 128 * half_at == row_b).astype(
                jnp.float32
            )
        return carry

    lax.fori_loop(0, TILES, mask_body, 0, unroll=4)
    picked = jnp.concatenate([hot_t[0].T, hot_t[1].T], axis=0)[0:ROWS].astype(jnp.bfloat16)
    hot[:, 0:128] = picked
    hot[:, 128:256] = picked

    def put_columns(dest, first, values):
        def body(g, carry):
            rows = pl.ds(pl.multiple_of(g * 8, 8), 8)
            for k, value in enumerate(values(rows)):
                turned = value.T
                for x in range(BX):
                    dest[g * BX + x, first + k] = jnp.broadcast_to(
                        turned[:, x + 1 : x + 2], (BLK, BLK)
                    )
            return carry

        lax.fori_loop(0, BY * BZ, body, 0, unroll=4)

    put_columns(
        col_x, 0, lambda rows: [data[k, rows, :] - org[k] for k in range(3)] + [data[3, rows, :]]
    )

    def place_x(first, last):
        for side, x in ((0, 0), (1, BX + 1)):
            for c in range(first, last):
                data[c, plane(x), :] = xr0[side, c]

    xv.arrive()
    place_x(0, 4)
    hv = halo_exchange(data, zs0, 0, 4)
    hv.start()
    put_columns(
        col_y,
        0,
        lambda rows: [(data[k, rows, :] - org[k]) + data[4 + k, rows, :] for k in range(3)],
    )
    xu.arrive()
    place_x(4, 7)
    hu = halo_exchange(data, zs0, 4, 7)
    hu.start()
    volume = data[3, 0:OWN_ROWS]
    inv[...] = jnp.where(volume > 0.0, 1.0 / jnp.where(volume > 0.0, volume, 1.0), 0.0)
    hv.arrive()
    for k in range(3):
        xrel[k] = data[k] - org[k]
    xrel[3] = data[3]

    def far_row(ref, k, at):
        return ref[k, pl.ds(at, 1), :]

    def put_sums(t, c, values, far_sign=1):
        near = jnp.sum(values.T.reshape(16, 8, BLK), axis=0)
        far = jnp.sum(values.reshape(16, 8, BLK), axis=0)
        first = pl.multiple_of(t * 16, 16)
        terms[c, pl.ds(first, 8), :] = near
        terms[c, pl.ds(first + 8, 8), :] = far if far_sign > 0 else -far

    def gather_sums(sums, channels):
        added = []
        for c in range(channels):
            total = terms[c, pl.ds(0, 2 * TILES, stride=8), :]
            for q in range(1, 8):
                total = total + terms[c, pl.ds(q, 2 * TILES, stride=8), :]
            added.append(total)
        full = jnp.concatenate(added, axis=1)
        high = full.astype(jnp.bfloat16)
        low = (full - high.astype(jnp.float32)).astype(jnp.bfloat16)
        rest = jnp.zeros((128 - 2 * TILES, channels * 128), jnp.bfloat16)
        out = jnp.dot(
            hot[...],
            jnp.concatenate([high, rest, low, rest], axis=0),
            preferred_element_type=jnp.float32,
        )
        for c in range(channels):
            sums[c] = out[:, c * 128 : (c + 1) * 128]

    def deformed(near, at):
        d = [far_row(ypos, k, at) - col_y[near, k] for k in range(3)]
        square = jnp.maximum(d[0] * d[0] + d[1] * d[1] + d[2] * d[2], TINY)
        inverse = lax.rsqrt(square)
        return d, square * inverse, inverse

    def rest_body(t, carry):
        near, at = near_at[t], far_at[t]
        o = [far_row(xrel, k, at) - col_x[near, k] for k in range(3)]
        square = jnp.maximum(o[0] * o[0] + o[1] * o[1] + o[2] * o[2], TINY)
        rest = square * lax.rsqrt(square)
        weight = w_ref[t] * (col_x[near, 3] * far_row(xrel, 3, at))
        w_ref[t] = weight
        r_ref[t] = rest
        put_sums(t, 0, weight * rest * rest)
        return carry

    def sum_body(t, carry):
        near, at = near_at[t], far_at[t]
        _, length, _ = deformed(near, at)
        rest = r_ref[t]
        put_sums(t, 0, w_ref[t] * rest * (length - rest))
        return carry

    def geometry_body(t, carry):
        near, at = near_at[t], far_at[t]
        d, length, inverse = deformed(near, at)
        e_ref[t] = length - r_ref[t]
        scale = w_ref[t] * inverse
        for k in range(3):
            n_ref[t, k] = scale * d[k]
        return carry

    def force_body(far_p, t, carry):
        near, at = near_at[t], far_at[t]
        c = r_ref[t] * (col_c[near, 0] + far_row(far_p, 0, at))
        c = c + e_ref[t] * (col_c[near, 1] + far_row(kapq, 1, at))
        for k in range(3):
            put_sums(t, k, c * n_ref[t, k], far_sign=-1)
        return carry

    def tiles(body):
        lax.fori_loop(0, TILES, body, 0, unroll=UNROLL)

    own_rows, ghost_rows = slice(0, OWN_ROWS), slice(OWN_ROWS, ROWS)

    def total_of(tot, sums, fold, fold_way, buffers, packed, xs, xr):
        send, recv = buffers
        fold_way.arrive()
        add_folds(tot, sums, fold, 1)
        pack_x(xs, tot, 1)
        main = x_exchange(xs, xr, 0, 1)
        main.start()
        pack_diagonal(send, tot)
        diagonal = diagonal_exchange(send, recv)
        diagonal.start()
        halo = halo_exchange(tot, packed, 0, 1)
        halo.start()
        return main, diagonal, halo

    tiles(rest_body)
    gather_sums(sum_m, 1)
    fm = fold_exchange(sum_m, fold_m)
    fm.start()
    hu.arrive()
    for k in range(3):
        ypos[k] = xrel[k] + data[4 + k]
    tiles(sum_body)
    gather_sums(sum_s1, 1)
    fs = fold_exchange(sum_s1, fold_s1)
    fs.start()
    fm.arrive()
    add_folds(sum_m, sum_m, fold_m, 1)
    pack_x(xsm, sum_m, 1)
    xm = x_exchange(xsm, xrm, 0, 1)
    xm.start()
    buffers = ((zf1, yf1, cf1), (zg1, yg1, cg1))
    main, diagonal, halo = total_of(tot1, sum_s1, fold_s1, fs, buffers, zs1, xs1, xr1)
    tiles(geometry_body)
    xm.arrive()
    add_x(sum_m, xrm, 1)
    floored = jnp.maximum(sum_m[0, own_rows] * inv[...], VOLUME_FLOOR)
    kapq[0, own_rows] = (3.0 * (3.0 * K_BULK - 5.0 * MU_SHEAR)) * inv[...] / floored / floored
    kapq[1, own_rows] = 15.0 * MU_SHEAR / floored
    hm = halo_exchange(kapq, zsm, 0, 2)
    hm.start()
    put_columns(col_c, 1, lambda rows: [kapq[1, rows, :]])

    def finish_total(tot, way, recv, coef, xr, kapq_halo=None):
        main, diagonal, halo = way
        main.arrive()
        halo.finish()
        pending.remove(halo)
        add_x(tot, xr, 1)
        coef[0, own_rows] = tot[0, own_rows] * kapq[0, own_rows]
        put_columns(col_c, 0, lambda rows: [coef[0, rows, :]])
        halo.arrive()
        diagonal.arrive()
        add_diagonal(tot, recv)
        if kapq_halo is not None:
            kapq_halo.arrive()
        coef[0, ghost_rows] = tot[0, ghost_rows] * kapq[0, ghost_rows]

    finish_total(tot1, (main, diagonal, halo), buffers[1], coef1, xr1, hm)
    xb.start()

    tiles(functools.partial(force_body, coef1))
    gather_sums(sum_f1, 3)
    f = fold_exchange(sum_f1, fold_f1)
    f.start()
    f.arrive()
    add_folds(sum_f1, sum_f1, fold_f1, 3)
    pack_x(xs2, sum_f1, 3)
    x2 = x_exchange(xs2, xr2, 0, 3)
    x2.start()
    xb.arrive()
    for side, x in ((0, 0), (1, BX + 1)):
        for k in range(3):
            base[k, plane(x), :] = xrb[side, k]
    pending.remove(x2)
    settle()
    pending.append(x2)
    x2.arrive()
    add_x(sum_f1, xr2, 3)
    for k in range(3):
        force = sum_f1[k, own_rows] * inv[...]
        sum_f1[k, own_rows] = force
        disp2[k, own_rows] = base[k] + (TIME_DELTA * TIME_DELTA) * force
    h2 = halo_exchange(disp2, zs2, 0, 3)
    h2.start()
    put_columns(
        col_y, 0, lambda rows: [xrel[k, rows, :] + disp2[k, rows, :] for k in range(3)]
    )
    for x in range(BX):
        for k in range(3):
            half[k, x] = half[k, x] + TIME_DELTA * sum_f1[k, plane(x + 1), :]
    h2.arrive()
    for k in range(3):
        ypos[k] = xrel[k] + disp2[k]

    tiles(sum_body)
    gather_sums(sum_s2, 1)
    fs = fold_exchange(sum_s2, fold_s2)
    fs.start()
    buffers = ((zf2, yf2, cf2), (zg2, yg2, cg2))
    way = total_of(tot2, sum_s2, fold_s2, fs, buffers, zs3, xs3, xr3)
    tiles(geometry_body)
    finish_total(tot2, way, buffers[1], coef2, xr3)

    tiles(functools.partial(force_body, coef2))
    gather_sums(sum_f2, 3)
    f = fold_exchange(sum_f2, fold_f2)
    f.start()
    f.arrive()
    add_folds(sum_f2, sum_f2, fold_f2, 3)
    for side, x in ((0, 0), (1, BX + 1)):
        for k in range(3):
            xs4[side, k] = sum_f2[k, plane(x), :]
    x4 = x_exchange(xs4, xr4, 0, 3)
    x4.start()
    pending.remove(x4)
    out_v[...] = half[...]
    for x in range(BX):
        for k in range(3):
            out_u[k, x] = disp2[k, plane(x + 1), :]
    settle()
    x4.arrive()
    for x in range(BX):
        for k in range(3):
            force = sum_f2[k, plane(x + 1), :]
            if x == 0:
                force = force + xr4[0, k]
            if x == BX - 1:
                force = force + xr4[1, k]
            force = force * inv[plane(x + 1), :]
            out_a[k, x] = force
    x4.finish()


def finish_kernel(u, h, a, out_u, out_v, out_a):
    out_u[...] = u[...]
    out_v[...] = h[...] + 0.5 * TIME_DELTA * a[...]
    out_a[...] = a[...]


def per_device(
    positions,
    volume,
    displacement,
    velocity,
    acceleration,
    tile_own,
    tile_partner,
    tile_count,
    family_bits,
    broken_bits,
):
    vmem = pl.BlockSpec(memory_space=pltpu.VMEM)
    smem = pl.BlockSpec(memory_space=pltpu.SMEM)
    hbm = pl.BlockSpec(memory_space=pl.ANY)
    out = jax.ShapeDtypeStruct((3, BX, BY * BZ, BLK), jnp.float32)

    def buf(*shape, dtype=jnp.float32):
        return pltpu.VMEM(shape, dtype)

    def grid(channels):
        return buf(channels, ROWS, BLK)

    def fold(channels):
        return buf(channels, ROWS - OWN_ROWS, BLK)

    def pair(channels, rows):
        return [buf(2, channels, rows, BLK), buf(2, channels, rows, BLK)]

    def diagonals():
        return [buf(2, 2, 8, BLK), buf(2, 2, 4, BLK), buf(2, 4, 2, BLK)]

    bits = pltpu.VMEM((TILES, WORDS, BLK), jnp.int32)
    copies = 11 * len(YZ) + 8 * 2 + 2 * 16
    values = (positions, displacement, velocity, acceleration)
    pos, dis, vel, acc = (v.reshape(3, BX, BY * BZ, BLK) for v in values)
    outs = pl.pallas_call(
        kernel,
        out_shape=[out] * 3,
        in_specs=[vmem] * 5 + [smem] * 3 + [hbm] * 2,
        out_specs=[vmem] * 3,
        scratch_shapes=[
            bits,
            bits,
            pltpu.SMEM((TILES,), jnp.int32),
            pltpu.SMEM((TILES,), jnp.int32),
            grid(7),
            grid(4),
            grid(3),
            buf(3, BX, BY * BZ, BLK),
            buf(3, OWN_ROWS, BLK),
            buf(OWN_ROWS, BLK),
            buf(TILES, BLK, BLK),
            buf(TILES, BLK, BLK),
            buf(TILES, BLK, BLK),
            buf(TILES, 3, BLK, BLK),
            buf(BX * BY * BZ, 4, BLK, BLK),
            buf(BX * BY * BZ, 3, BLK, BLK),
            buf(BX * BY * BZ, 2, BLK, BLK),
            buf(2, 128, 128),
            buf(ROWS, 256, dtype=jnp.bfloat16),
            buf(3, TILES * 16, 128),
            grid(1),
            grid(1),
            grid(3),
            grid(1),
            grid(3),
            grid(1),
            grid(1),
            grid(2),
            grid(1),
            grid(1),
            grid(3),
            fold(1),
            fold(1),
            fold(3),
            fold(1),
            fold(3),
            buf(2, 7, BY * 8, BLK),
            buf(2, 2, BY * 8, BLK),
            buf(2, 1, BY * 8, BLK),
            buf(2, 3, BY * 8, BLK),
            buf(2, 1, BY * 8, BLK),
            *pair(7, 8),
            *pair(3, 8),
            *pair(1, 16),
            *pair(1, 16),
            *pair(3, 16),
            *pair(1, 16),
            *pair(3, 8),
            *diagonals(),
            *diagonals(),
            *diagonals(),
            *diagonals(),
            pltpu.SemaphoreType.DMA((copies,)),
            pltpu.SemaphoreType.DMA((copies,)),
            pltpu.SemaphoreType.DMA((2,)),
        ],
        compiler_params=pltpu.CompilerParams(
            collective_id=0, has_side_effects=True, vmem_limit_bytes=56 * 1024 * 1024
        ),
    )(
        pos,
        volume.reshape(BX, BY * BZ, BLK),
        dis,
        vel,
        acc,
        tile_own.reshape(TILES),
        tile_partner.reshape(TILES),
        tile_count,
        family_bits.reshape(TILES, WORDS, BLK),
        broken_bits.reshape(TILES, WORDS, BLK),
    )
    outs = pl.pallas_call(
        finish_kernel, out_shape=[out] * 3, in_specs=[vmem] * 3, out_specs=[vmem] * 3
    )(*outs)
    return tuple(v.reshape(3, BX, BY, BZ, BLK) for v in outs)


def solution(mesh):
    in_specs = (
        P(None, "gx", "gy", "gz", None),
        P("gx", "gy", "gz", None),
        P(None, "gx", "gy", "gz", None),
        P(None, "gx", "gy", "gz", None),
        P(None, "gx", "gy", "gz", None),
        P("gx", "gy", "gz", None),
        P("gx", "gy", "gz", None),
        P("gx", "gy", "gz"),
        P("gx", "gy", "gz", None, None, None),
        P("gx", "gy", "gz", None, None, None),
    )
    out_specs = (
        P(None, "gx", "gy", "gz", None),
        P(None, "gx", "gy", "gz", None),
        P(None, "gx", "gy", "gz", None),
    )
    return jax.shard_map(
        per_device, mesh=mesh, in_specs=in_specs, out_specs=out_specs, check_vma=False
    )
```

```python
import functools

import jax
import jax.numpy as jnp
from jax import lax
from jax.experimental import pallas as pl
from jax.experimental.pallas import tpu as pltpu
from jax.sharding import PartitionSpec as P

BLK = 128
WORDS = 16
BX, BY, BZ = 4, 4, 2
TILES = 40
N_DEV = 8
K_BULK = 8000.0
MU_SHEAR = 600.0
VOLUME_FLOOR = 2000.0
TIME_DELTA = 0.05
TINY = 1e-30
UNROLL = 8
ROWS = (BY + 2) * (BZ + 2) * 8

YZ = [(-1, 0), (1, 0), (0, -1), (0, 1), (-1, -1), (-1, 1), (1, -1), (1, 1)]
OWN_ROWS = BY * BZ * 8
GHOST = dict(zip(YZ, (slice(64, 80), slice(80, 96), slice(96, 128), slice(128, 160), slice(160, 168), slice(168, 176), slice(176, 184), slice(184, 192))))
INNER = {
    (-1, 0): (0, 1),
    (1, 0): (6, 7),
    (0, -1): (0, 2, 4, 6),
    (0, 1): (1, 3, 5, 7),
    (-1, -1): (0,),
    (-1, 1): (1,),
    (1, -1): (6,),
    (1, 1): (7,),
}


def slot(step):
    rows = GHOST[step]
    return slice(rows.start - OWN_ROWS, rows.stop - OWN_ROWS)


def column(g):
    return slice(g * 8, g * 8 + 8)


def plane(x):
    return pl.ds(x, 8, stride=8)


def kernel(
    pos_hbm,
    vol_hbm,
    dis_hbm,
    vel_hbm,
    acc_hbm,
    own,
    par,
    cnt,
    fam_hbm,
    brk_hbm,
    u_hbm,
    v_hbm,
    a_hbm,
    pos,
    vol,
    dis,
    vel,
    acc,
    out_u,
    out_v,
    out_a,
    fam,
    brk,
    near_at,
    far_at,
    data,
    xrel,
    ypos,
    half,
    base,
    inv,
    w_ref,
    r_ref,
    e_ref,
    n_ref,
    col_x,
    col_y,
    col_c,
    hot_t,
    hot,
    terms,
    sum_m,
    sum_s1,
    sum_f1,
    sum_s2,
    sum_f2,
    tot1,
    tot2,
    kapq,
    coef1,
    coef2,
    disp2,
    fold_m,
    fold_s1,
    fold_f1,
    fold_s2,
    fold_f2,
    zs0,
    zsm,
    zs1,
    zs2,
    zs3,
    xs0,
    xr0,
    xsb,
    xrb,
    xsm,
    xrm,
    xs1,
    xr1,
    xs2,
    xr2,
    xs3,
    xr3,
    xs4,
    xr4,
    zf1,
    yf1,
    cf1,
    zg1,
    yg1,
    cg1,
    zf2,
    yf2,
    cf2,
    zg2,
    yg2,
    cg2,
    zf4,
    yf4,
    cf4,
    zg4,
    yg4,
    cg4,
    send_sem,
    recv_sem,
    load_sem,
):
    gx, gy, gz = lax.axis_index("gx"), lax.axis_index("gy"), lax.axis_index("gz")
    counter = [0]
    pending = []

    def there(step):
        ok = None
        for at, d in zip((gx, gy, gz), step):
            if d:
                test = at > 0 if d < 0 else at < N_DEV - 1
                ok = test if ok is None else jnp.logical_and(ok, test)
        return ok

    def target(step):
        return tuple(at + d for at, d in zip((gx, gy, gz), step))

    class Exchange:
        def __init__(self, steps, source, sink):
            self.steps, self.base = steps, counter[0]
            counter[0] += len(steps)
            self.source, self.sink = source, sink
            pending.append(self)

        def copy(self, i, step, back):
            opposite = tuple(-d for d in step)
            return pltpu.make_async_remote_copy(
                src_ref=self.source(step),
                dst_ref=self.sink(step if back else opposite),
                send_sem=send_sem.at[self.base + i],
                recv_sem=recv_sem.at[self.base + (i if back else self.steps.index(opposite))],
                device_id=target(step),
                device_id_type=pl.DeviceIdType.MESH,
            )

        def start(self):
            for i, step in enumerate(self.steps):
                pl.when(there(step))(lambda i=i, step=step: self.copy(i, step, False).start())

        def arrive(self):
            for i, step in enumerate(self.steps):
                pl.when(there(step))(lambda i=i, step=step: self.copy(i, step, True).wait_recv())

        def finish(self):
            for i, step in enumerate(self.steps):
                pl.when(there(step))(lambda i=i, step=step: self.copy(i, step, False).wait_send())

    def settle():
        while pending:
            pending.pop(0).finish()

    yz_steps = [(0, dy, dz) for dy, dz in YZ]
    diagonal_steps = [(dx, dy, dz) for dx in (-1, 1) for dy, dz in YZ]
    x_steps = [(-1, 0, 0), (1, 0, 0)]

    def fold_exchange(sums, fold):
        return Exchange(
            yz_steps,
            lambda s: sums.at[:, GHOST[s[1:]]],
            lambda s: fold.at[:, slot(s[1:])],
        )

    def add_folds(dest, sums, fold, channels):
        for c in range(channels):
            for g in range(BY * BZ):
                total = sums[c, column(g)]
                for step in YZ:
                    if g in INNER[step]:
                        first = slot(step).start + INNER[step].index(g) * 8
                        total = total + fold[c, first : first + 8]
                dest[c, column(g)] = total

    def halo_exchange(array, packed, first, last):
        def source(s):
            step = s[1:]
            if step[0] == 0:
                return packed.at[(step[1] + 1) // 2, first:last]
            groups = INNER[step]
            return array.at[first:last, groups[0] * 8 : groups[-1] * 8 + 8]

        for side in (0, 1):
            for j in range(BY):
                for c in range(first, last):
                    packed[side, c, column(j)] = array[c, column(2 * j + side)]
        return Exchange(yz_steps, source, lambda s: array.at[first:last, GHOST[s[1:]]])

    def x_exchange(send, recv, first, last):
        return Exchange(
            x_steps,
            lambda s: send.at[(s[0] + 1) // 2, first:last],
            lambda s: recv.at[(s[0] + 1) // 2, first:last],
        )

    def diagonal_exchange(send, recv):
        def of(buffers, s):
            faces_z, faces_y, corners = buffers
            x, y, z = ((d + 1) // 2 for d in s)
            if s[1] == 0:
                return faces_z.at[x, z]
            return faces_y.at[x, y] if s[2] == 0 else corners.at[x, 2 * y + z]

        return Exchange(diagonal_steps, lambda s: of(send, s), lambda s: of(recv, s))

    def pack_diagonal(send, array):
        faces_z, faces_y, corners = send
        for side in (0, 1):
            for j, x in enumerate(shared(side)):
                for i in (0, 1):
                    faces_z[side, i, j * 4 : j * 4 + 4] = array[0, pl.ds(8 * i + x, 4, stride=16), :]
                    faces_y[side, i, j * 2 : j * 2 + 2] = array[0, pl.ds(48 * i + x, 2, stride=8), :]
                for i, g in enumerate((0, 1, 6, 7)):
                    corners[side, i, j : j + 1] = array[0, pl.ds(g * 8 + x, 1), :]

    def add_diagonal(array, recv):
        faces_z, faces_y, corners = recv
        for side in (0, 1):
            for j, x in enumerate(shared(side)):
                for i, d in enumerate((-1, 1)):
                    at = pl.ds(GHOST[(0, d)].start + x, 4, stride=8)
                    array[0, at, :] = array[0, at, :] + faces_z[side, i, j * 4 : j * 4 + 4]
                    at = pl.ds(GHOST[(d, 0)].start + x, 2, stride=8)
                    array[0, at, :] = array[0, at, :] + faces_y[side, i, j * 2 : j * 2 + 2]
                for i in range(4):
                    at = pl.ds(GHOST[(i // 2 * 2 - 1, i % 2 * 2 - 1)].start + x, 1)
                    array[0, at, :] = array[0, at, :] + corners[side, i, j : j + 1]

    def shared(side):
        return ((0, 1), (BX, BX + 1))[side]

    def pack_x(send, array, channels):
        for side in (0, 1):
            for c in range(channels):
                for j, x in enumerate(shared(side)):
                    send[side, c, column(j)] = array[c, plane(x), :]

    def add_x(array, recv, channels):
        for side in (0, 1):
            for c in range(channels):
                for j, x in enumerate(shared(side)):
                    array[c, plane(x), :] = array[c, plane(x), :] + recv[side, c, column(j)]

    barrier = pltpu.get_barrier_semaphore()
    expected = jnp.int32(0)
    for step in x_steps + yz_steps + diagonal_steps:
        expected = expected + there(step).astype(jnp.int32)

        @pl.when(there(step))
        def _(step=step):
            pl.semaphore_signal(
                barrier, inc=1, device_id=target(step), device_id_type=pl.DeviceIdType.MESH
            )

    pairs = (
        (pos_hbm, pos),
        (vol_hbm, vol),
        (dis_hbm, dis),
        (vel_hbm, vel),
        (acc_hbm, acc),
        (fam_hbm, fam),
        (brk_hbm, brk),
        (out_u, u_hbm),
        (out_v, v_hbm),
        (out_a, a_hbm),
    )
    moves = [pltpu.make_async_copy(a, b, load_sem.at[i]) for i, (a, b) in enumerate(pairs)]
    loads, stores = moves[:7], moves[7:]
    for load in loads:
        load.start()

    loads[0].wait()
    loads[1].wait()
    for side, x in ((0, 0), (1, BX - 1)):
        xs0[side, 3] = vol[x]
        for k in range(3):
            xs0[side, k] = pos[k, x]
    pl.semaphore_wait(barrier, expected)
    xv = x_exchange(xs0, xr0, 0, 4)
    xv.start()
    for load in loads[2:5]:
        load.wait()
    for x in (0, BX - 1, 1, 2):
        for k in range(3):
            h = vel[k, x] + 0.5 * TIME_DELTA * acc[k, x]
            u1 = dis[k, x] + TIME_DELTA * h
            data[4 + k, plane(x + 1), :] = u1
            half[k, x] = h
            base[k, plane(x + 1), :] = u1 + TIME_DELTA * h
            if x == 0 or x == BX - 1:
                xs0[x // (BX - 1), 4 + k] = u1
                xsb[x // (BX - 1), k] = u1 + TIME_DELTA * h
    xu = x_exchange(xs0, xr0, 4, 7)
    xb = x_exchange(xsb, xrb, 0, 3)
    xu.start()
    for x in range(BX):
        data[3, plane(x + 1), :] = vol[x]
        for k in range(3):
            data[k, plane(x + 1), :] = pos[k, x]

    for side, step in enumerate(x_steps):

        @pl.when(jnp.logical_not(there(step)))
        def _(side=side):
            for ref in (xr0, xrb, xrm, xr1, xr2, xr3, xr4):
                ref[side] = jnp.zeros(ref.shape[1:], jnp.float32)

    for step in diagonal_steps:

        @pl.when(jnp.logical_not(there(step)))
        def _(step=step):
            x, y, z = ((d + 1) // 2 for d in step)
            for faces_z, faces_y, corners in ((zg1, yg1, cg1), (zg2, yg2, cg2)):
                if step[1] == 0:
                    faces_z[x, z] = jnp.zeros((8, BLK), jnp.float32)
                elif step[2] == 0:
                    faces_y[x, y] = jnp.zeros((4, BLK), jnp.float32)
                else:
                    corners[x, 2 * y + z] = jnp.zeros((2, BLK), jnp.float32)
            if step[1] == 0:
                zg4[x, z] = jnp.zeros((3, 4, BLK), jnp.float32)
            elif step[2] == 0:
                yg4[x, y] = jnp.zeros((3, 2, BLK), jnp.float32)
            else:
                cg4[x, 2 * y + z] = jnp.zeros((3, 1, BLK), jnp.float32)

    for step in YZ:

        @pl.when(jnp.logical_not(there((0,) + step)))
        def _(step=step):
            for ref in (data, kapq, disp2, tot1, tot2):
                rows = GHOST[step]
                ref[:, rows] = jnp.zeros((ref.shape[0], rows.stop - rows.start, BLK), jnp.float32)
            for ref in (fold_m, fold_s1, fold_f1, fold_s2, fold_f2):
                rows = slot(step)
                ref[:, rows] = jnp.zeros((ref.shape[0], rows.stop - rows.start, BLK), jnp.float32)

    hot_t[...] = jnp.zeros_like(hot_t)
    org = [g.astype(jnp.float32) * 16.0 for g in (gx, gy, gz)]
    loads[5].wait()
    loads[6].wait()
    sub = lax.broadcasted_iota(jnp.int32, (BLK, BLK), 0)
    lane = lax.broadcasted_iota(jnp.int32, (BLK, BLK), 1)

    def row_of(block):
        x, g = block // 24, block % 24
        y, z = g // 4, g % 4
        inside_y, inside_z = (y >= 1) & (y <= BY), (z >= 1) & (z <= BZ)
        upper_y, upper_z = (y > BY).astype(jnp.int32), (z > BZ).astype(jnp.int32)
        at_y = jnp.where(inside_z, 8 + 2 * upper_y + z - 1, 20 + 2 * upper_y + upper_z)
        in_y = jnp.where(inside_z, (y - 1) * 2 + z - 1, 12 + 4 * upper_z + y - 1)
        return jnp.where(inside_y, in_y, at_y) * 8 + x

    def mask_body(t, carry):
        a, b = own[t], par[t]
        row_a, row_b = row_of(a), row_of(b)
        near_at[t] = jnp.clip(row_a // 8 * BX + row_a % 8 - 1, 0, BX * BY * BZ - 1)
        far_at[t] = jnp.clip(row_b, 0, ROWS - 1)
        apart = (a != b).astype(jnp.int32)
        live = (t < cnt[0, 0, 0]).astype(jnp.int32)
        shift = lax.broadcasted_iota(jnp.int32, (8, BLK), 0)
        rows = []
        for g in range(WORDS):
            word = fam[t, pl.ds(g, 1), :] & ~brk[t, pl.ds(g, 1), :]
            rows.append((jnp.broadcast_to(word, (8, BLK)) >> shift) & 1)
        bits = jnp.concatenate(rows, axis=0)
        bits = bits & ((sub > lane).astype(jnp.int32) | apart) & live
        w_ref[t] = bits.astype(jnp.float32).T
        code = lax.broadcasted_iota(jnp.int32, (1, BLK), 1)
        for half_at in range(2):
            hot_t[half_at, pl.ds(2 * t, 1), :] = (code + 128 * half_at == row_a).astype(jnp.float32)
            hot_t[half_at, pl.ds(2 * t + 1, 1), :] = (code + 128 * half_at == row_b).astype(
                jnp.float32
            )
        return carry

    lax.fori_loop(0, TILES, mask_body, 0, unroll=4)
    picked = jnp.concatenate([hot_t[0].T, hot_t[1].T], axis=0)[0:ROWS].astype(jnp.bfloat16)
    hot[:, 0:128] = picked
    hot[:, 128:256] = picked

    def put_columns(dest, first, values):
        def body(g, carry):
            rows = pl.ds(pl.multiple_of(g * 8, 8), 8)
            for k, value in enumerate(values(rows)):
                turned = value.T
                for x in range(BX):
                    dest[g * BX + x, first + k] = jnp.broadcast_to(
                        turned[:, x + 1 : x + 2], (BLK, BLK)
                    )
            return carry

        lax.fori_loop(0, BY * BZ, body, 0, unroll=4)

    put_columns(
        col_x, 0, lambda rows: [data[k, rows, :] - org[k] for k in range(3)] + [data[3, rows, :]]
    )

    def place_x(first, last):
        for side, x in ((0, 0), (1, BX + 1)):
            for c in range(first, last):
                data[c, plane(x), :] = xr0[side, c]

    xv.arrive()
    place_x(0, 4)
    hv = halo_exchange(data, zs0, 0, 4)
    hv.start()
    put_columns(
        col_y,
        0,
        lambda rows: [(data[k, rows, :] - org[k]) + data[4 + k, rows, :] for k in range(3)],
    )
    xu.arrive()
    place_x(4, 7)
    hu = halo_exchange(data, zs0, 4, 7)
    hu.start()
    volume = data[3, 0:OWN_ROWS]
    inv[...] = jnp.where(volume > 0.0, 1.0 / jnp.where(volume > 0.0, volume, 1.0), 0.0)
    hv.arrive()
    for k in range(3):
        xrel[k] = data[k] - org[k]
    xrel[3] = data[3]

    def far_row(ref, k, at):
        return ref[k, pl.ds(at, 1), :]

    def put_sums(t, c, values, far_sign=1):
        near = jnp.sum(values.T.reshape(16, 8, BLK), axis=0)
        far = jnp.sum(values.reshape(16, 8, BLK), axis=0)
        first = pl.multiple_of(t * 16, 16)
        terms[c, pl.ds(first, 8), :] = near
        terms[c, pl.ds(first + 8, 8), :] = far if far_sign > 0 else -far

    def gather_sums(sums, channels):
        added = []
        for c in range(channels):
            total = terms[c, pl.ds(0, 2 * TILES, stride=8), :]
            for q in range(1, 8):
                total = total + terms[c, pl.ds(q, 2 * TILES, stride=8), :]
            added.append(total)
        full = jnp.concatenate(added, axis=1)
        high = full.astype(jnp.bfloat16)
        low = (full - high.astype(jnp.float32)).astype(jnp.bfloat16)
        rest = jnp.zeros((128 - 2 * TILES, channels * 128), jnp.bfloat16)
        out = jnp.dot(
            hot[...],
            jnp.concatenate([high, rest, low, rest], axis=0),
            preferred_element_type=jnp.float32,
        )
        for c in range(channels):
            sums[c] = out[:, c * 128 : (c + 1) * 128]

    def deformed(near, at):
        d = [far_row(ypos, k, at) - col_y[near, k] for k in range(3)]
        square = jnp.maximum(d[0] * d[0] + d[1] * d[1] + d[2] * d[2], TINY)
        inverse = lax.rsqrt(square)
        return d, square * inverse, inverse

    def rest_body(t, carry):
        near, at = near_at[t], far_at[t]
        o = [far_row(xrel, k, at) - col_x[near, k] for k in range(3)]
        square = jnp.maximum(o[0] * o[0] + o[1] * o[1] + o[2] * o[2], TINY)
        rest = square * lax.rsqrt(square)
        weight = w_ref[t] * (col_x[near, 3] * far_row(xrel, 3, at))
        w_ref[t] = weight
        r_ref[t] = rest
        put_sums(t, 0, weight * rest * rest)
        return carry

    def sum_body(t, carry):
        near, at = near_at[t], far_at[t]
        _, length, _ = deformed(near, at)
        rest = r_ref[t]
        put_sums(t, 0, w_ref[t] * rest * (length - rest))
        return carry

    def geometry_body(t, carry):
        near, at = near_at[t], far_at[t]
        d, length, inverse = deformed(near, at)
        e_ref[t] = length - r_ref[t]
        scale = w_ref[t] * inverse
        for k in range(3):
            n_ref[t, k] = scale * d[k]
        return carry

    def force_body(far_p, t, carry):
        near, at = near_at[t], far_at[t]
        c = r_ref[t] * (col_c[near, 0] + far_row(far_p, 0, at))
        c = c + e_ref[t] * (col_c[near, 1] + far_row(kapq, 1, at))
        for k in range(3):
            put_sums(t, k, c * n_ref[t, k], far_sign=-1)
        return carry

    def tiles(body):
        lax.fori_loop(0, TILES, body, 0, unroll=UNROLL)

    own_rows, ghost_rows = slice(0, OWN_ROWS), slice(OWN_ROWS, ROWS)

    def total_of(tot, sums, fold, fold_way, buffers, packed, xs, xr):
        send, recv = buffers
        fold_way.arrive()
        add_folds(tot, sums, fold, 1)
        pack_x(xs, tot, 1)
        main = x_exchange(xs, xr, 0, 1)
        main.start()
        pack_diagonal(send, tot)
        diagonal = diagonal_exchange(send, recv)
        diagonal.start()
        halo = halo_exchange(tot, packed, 0, 1)
        halo.start()
        return main, diagonal, halo

    tiles(rest_body)
    gather_sums(sum_m, 1)
    fm = fold_exchange(sum_m, fold_m)
    fm.start()
    hu.arrive()
    for k in range(3):
        ypos[k] = xrel[k] + data[4 + k]
    tiles(sum_body)
    gather_sums(sum_s1, 1)
    fs = fold_exchange(sum_s1, fold_s1)
    fs.start()
    fm.arrive()
    add_folds(sum_m, sum_m, fold_m, 1)
    pack_x(xsm, sum_m, 1)
    xm = x_exchange(xsm, xrm, 0, 1)
    xm.start()
    buffers = ((zf1, yf1, cf1), (zg1, yg1, cg1))
    main, diagonal, halo = total_of(tot1, sum_s1, fold_s1, fs, buffers, zs1, xs1, xr1)
    tiles(geometry_body)
    xm.arrive()
    add_x(sum_m, xrm, 1)
    floored = jnp.maximum(sum_m[0, own_rows] * inv[...], VOLUME_FLOOR)
    kapq[0, own_rows] = (3.0 * (3.0 * K_BULK - 5.0 * MU_SHEAR)) * inv[...] / floored / floored
    kapq[1, own_rows] = 15.0 * MU_SHEAR / floored
    hm = halo_exchange(kapq, zsm, 0, 2)
    hm.start()
    put_columns(col_c, 1, lambda rows: [kapq[1, rows, :]])

    def finish_total(tot, way, recv, coef, xr, kapq_halo=None):
        main, diagonal, halo = way
        main.arrive()
        halo.finish()
        pending.remove(halo)
        add_x(tot, xr, 1)
        coef[0, own_rows] = tot[0, own_rows] * kapq[0, own_rows]
        put_columns(col_c, 0, lambda rows: [coef[0, rows, :]])
        halo.arrive()
        diagonal.arrive()
        add_diagonal(tot, recv)
        if kapq_halo is not None:
            kapq_halo.arrive()
        coef[0, ghost_rows] = tot[0, ghost_rows] * kapq[0, ghost_rows]

    finish_total(tot1, (main, diagonal, halo), buffers[1], coef1, xr1, hm)
    xb.start()

    tiles(functools.partial(force_body, coef1))
    gather_sums(sum_f1, 3)
    f = fold_exchange(sum_f1, fold_f1)
    f.start()
    f.arrive()
    add_folds(sum_f1, sum_f1, fold_f1, 3)
    pack_x(xs2, sum_f1, 3)
    x2 = x_exchange(xs2, xr2, 0, 3)
    x2.start()
    xb.arrive()
    for side, x in ((0, 0), (1, BX + 1)):
        for k in range(3):
            base[k, plane(x), :] = xrb[side, k]
    pending.remove(x2)
    settle()
    pending.append(x2)
    x2.arrive()
    add_x(sum_f1, xr2, 3)
    for k in range(3):
        force = sum_f1[k, own_rows] * inv[...]
        sum_f1[k, own_rows] = force
        disp2[k, own_rows] = base[k] + (TIME_DELTA * TIME_DELTA) * force
    h2 = halo_exchange(disp2, zs2, 0, 3)
    h2.start()
    put_columns(
        col_y, 0, lambda rows: [xrel[k, rows, :] + disp2[k, rows, :] for k in range(3)]
    )
    for x in range(BX):
        for k in range(3):
            half[k, x] = half[k, x] + TIME_DELTA * sum_f1[k, plane(x + 1), :]
    h2.arrive()
    for k in range(3):
        ypos[k] = xrel[k] + disp2[k]

    tiles(sum_body)
    gather_sums(sum_s2, 1)
    fs = fold_exchange(sum_s2, fold_s2)
    fs.start()
    buffers = ((zf2, yf2, cf2), (zg2, yg2, cg2))
    way = total_of(tot2, sum_s2, fold_s2, fs, buffers, zs3, xs3, xr3)
    tiles(geometry_body)
    finish_total(tot2, way, buffers[1], coef2, xr3)

    tiles(functools.partial(force_body, coef2))
    gather_sums(sum_f2, 3)
    for side, x in ((0, 0), (1, BX + 1)):
        for k in range(3):
            xs4[side, k] = sum_f2[k, plane(x), :]
    x4 = x_exchange(xs4, xr4, 0, 3)
    x4.start()
    for side, x in ((0, 0), (1, BX + 1)):
        for k in range(3):
            for i, d in enumerate((-1, 1)):
                at = pl.ds(GHOST[(0, d)].start + x, 4, stride=8)
                zf4[side, i, k] = sum_f2[k, at, :]
                at = pl.ds(GHOST[(d, 0)].start + x, 2, stride=8)
                yf4[side, i, k] = sum_f2[k, at, :]
            for i in range(4):
                at = pl.ds(GHOST[(i // 2 * 2 - 1, i % 2 * 2 - 1)].start + x, 1)
                cf4[side, i, k] = sum_f2[k, at, :]
    d4 = diagonal_exchange((zf4, yf4, cf4), (zg4, yg4, cg4))
    d4.start()
    f = fold_exchange(sum_f2, fold_f2)
    f.start()
    for way in (x4, d4, f):
        pending.remove(way)
    out_v[...] = half[...]
    for x in range(BX):
        for k in range(3):
            out_u[k, x] = disp2[k, plane(x + 1), :]
    stores[0].start()
    stores[1].start()
    settle()
    f.arrive()
    add_folds(sum_f2, sum_f2, fold_f2, 3)
    x4.arrive()
    d4.arrive()
    for side, x in ((0, 1), (1, BX)):
        for k in range(3):
            for i in (0, 1):
                at = pl.ds(8 * i + x, 4, stride=16)
                sum_f2[k, at, :] = sum_f2[k, at, :] + zg4[side, i, k]
                at = pl.ds(48 * i + x, 2, stride=8)
                sum_f2[k, at, :] = sum_f2[k, at, :] + yg4[side, i, k]
            for i, g in enumerate((0, 1, 6, 7)):
                at = pl.ds(g * 8 + x, 1)
                sum_f2[k, at, :] = sum_f2[k, at, :] + cg4[side, i, k]
    for x in range(BX):
        for k in range(3):
            force = sum_f2[k, plane(x + 1), :]
            if x == 0:
                force = force + xr4[0, k]
            if x == BX - 1:
                force = force + xr4[1, k]
            out_a[k, x] = force * inv[plane(x + 1), :]
    stores[2].start()
    for way in (x4, d4, f):
        way.finish()
    for store in stores:
        store.wait()


def finish_kernel(u, h, a, out_u, out_v, out_a):
    out_u[...] = u[...]
    out_v[...] = h[...] + 0.5 * TIME_DELTA * a[...]
    out_a[...] = a[...]


def per_device(
    positions,
    volume,
    displacement,
    velocity,
    acceleration,
    tile_own,
    tile_partner,
    tile_count,
    family_bits,
    broken_bits,
):
    vmem = pl.BlockSpec(memory_space=pltpu.VMEM)
    smem = pl.BlockSpec(memory_space=pltpu.SMEM)
    hbm = pl.BlockSpec(memory_space=pl.ANY)
    out = jax.ShapeDtypeStruct((3, BX, BY * BZ, BLK), jnp.float32)

    def buf(*shape, dtype=jnp.float32):
        return pltpu.VMEM(shape, dtype)

    def grid(channels):
        return buf(channels, ROWS, BLK)

    def fold(channels):
        return buf(channels, ROWS - OWN_ROWS, BLK)

    def pair(channels, rows):
        return [buf(2, channels, rows, BLK), buf(2, channels, rows, BLK)]

    def diagonals():
        return [buf(2, 2, 8, BLK), buf(2, 2, 4, BLK), buf(2, 4, 2, BLK)]

    def last_diagonals():
        return [buf(2, 2, 3, 4, BLK), buf(2, 2, 3, 2, BLK), buf(2, 4, 3, 1, BLK)]

    bits = pltpu.VMEM((TILES, WORDS, BLK), jnp.int32)
    copies = 11 * len(YZ) + 8 * 2 + 3 * 16
    points = buf(3, BX, BY * BZ, BLK)
    values = (positions, displacement, velocity, acceleration)
    pos, dis, vel, acc = (v.reshape(3, BX, BY * BZ, BLK) for v in values)
    outs = pl.pallas_call(
        kernel,
        out_shape=[out] * 3,
        in_specs=[hbm] * 5 + [smem] * 3 + [hbm] * 2,
        out_specs=[hbm] * 3,
        scratch_shapes=[
            points,
            buf(BX, BY * BZ, BLK),
            *[points] * 6,
            bits,
            bits,
            pltpu.SMEM((TILES,), jnp.int32),
            pltpu.SMEM((TILES,), jnp.int32),
            grid(7),
            grid(4),
            grid(3),
            buf(3, BX, BY * BZ, BLK),
            buf(3, OWN_ROWS, BLK),
            buf(OWN_ROWS, BLK),
            buf(TILES, BLK, BLK),
            buf(TILES, BLK, BLK),
            buf(TILES, BLK, BLK),
            buf(TILES, 3, BLK, BLK),
            buf(BX * BY * BZ, 4, BLK, BLK),
            buf(BX * BY * BZ, 3, BLK, BLK),
            buf(BX * BY * BZ, 2, BLK, BLK),
            buf(2, 128, 128),
            buf(ROWS, 256, dtype=jnp.bfloat16),
            buf(3, TILES * 16, 128),
            grid(1),
            grid(1),
            grid(3),
            grid(1),
            grid(3),
            grid(1),
            grid(1),
            grid(2),
            grid(1),
            grid(1),
            grid(3),
            fold(1),
            fold(1),
            fold(3),
            fold(1),
            fold(3),
            buf(2, 7, BY * 8, BLK),
            buf(2, 2, BY * 8, BLK),
            buf(2, 1, BY * 8, BLK),
            buf(2, 3, BY * 8, BLK),
            buf(2, 1, BY * 8, BLK),
            *pair(7, 8),
            *pair(3, 8),
            *pair(1, 16),
            *pair(1, 16),
            *pair(3, 16),
            *pair(1, 16),
            *pair(3, 8),
            *diagonals(),
            *diagonals(),
            *diagonals(),
            *diagonals(),
            *last_diagonals(),
            *last_diagonals(),
            pltpu.SemaphoreType.DMA((copies,)),
            pltpu.SemaphoreType.DMA((copies,)),
            pltpu.SemaphoreType.DMA((10,)),
        ],
        compiler_params=pltpu.CompilerParams(
            collective_id=0, has_side_effects=True, vmem_limit_bytes=56 * 1024 * 1024
        ),
    )(
        pos,
        volume.reshape(BX, BY * BZ, BLK),
        dis,
        vel,
        acc,
        tile_own.reshape(TILES),
        tile_partner.reshape(TILES),
        tile_count,
        family_bits.reshape(TILES, WORDS, BLK),
        broken_bits.reshape(TILES, WORDS, BLK),
    )
    outs = pl.pallas_call(
        finish_kernel, out_shape=[out] * 3, in_specs=[vmem] * 3, out_specs=[vmem] * 3
    )(*outs)
    return tuple(v.reshape(3, BX, BY, BZ, BLK) for v in outs)


def solution(mesh):
    in_specs = (
        P(None, "gx", "gy", "gz", None),
        P("gx", "gy", "gz", None),
        P(None, "gx", "gy", "gz", None),
        P(None, "gx", "gy", "gz", None),
        P(None, "gx", "gy", "gz", None),
        P("gx", "gy", "gz", None),
        P("gx", "gy", "gz", None),
        P("gx", "gy", "gz"),
        P("gx", "gy", "gz", None, None, None),
        P("gx", "gy", "gz", None, None, None),
    )
    out_specs = (
        P(None, "gx", "gy", "gz", None),
        P(None, "gx", "gy", "gz", None),
        P(None, "gx", "gy", "gz", None),
    )
    return jax.shard_map(
        per_device, mesh=mesh, in_specs=in_specs, out_specs=out_specs, check_vma=False
    )
```

```python
import functools

import jax
import jax.numpy as jnp
from jax import lax
from jax.experimental import pallas as pl
from jax.experimental.pallas import tpu as pltpu
from jax.sharding import PartitionSpec as P

BLK = 128
WORDS = 16
BX, BY, BZ = 4, 4, 2
TILES = 40
N_DEV = 8
K_BULK = 8000.0
MU_SHEAR = 600.0
VOLUME_FLOOR = 2000.0
TIME_DELTA = 0.05
TINY = 1e-30
UNROLL = 8
ROWS = (BY + 2) * (BZ + 2) * 8

YZ = [(-1, 0), (1, 0), (0, -1), (0, 1), (-1, -1), (-1, 1), (1, -1), (1, 1)]
OWN_ROWS = BY * BZ * 8
GHOST = dict(zip(YZ, (slice(64, 80), slice(80, 96), slice(96, 128), slice(128, 160), slice(160, 168), slice(168, 176), slice(176, 184), slice(184, 192))))
INNER = {
    (-1, 0): (0, 1),
    (1, 0): (6, 7),
    (0, -1): (0, 2, 4, 6),
    (0, 1): (1, 3, 5, 7),
    (-1, -1): (0,),
    (-1, 1): (1,),
    (1, -1): (6,),
    (1, 1): (7,),
}


def slot(step):
    rows = GHOST[step]
    return slice(rows.start - OWN_ROWS, rows.stop - OWN_ROWS)


def column(g):
    return slice(g * 8, g * 8 + 8)


def plane(x):
    return pl.ds(x, 8, stride=8)


def kernel(
    pos_hbm,
    vol_hbm,
    dis_hbm,
    vel_hbm,
    acc_hbm,
    own,
    par,
    cnt,
    fam_hbm,
    brk_hbm,
    u_hbm,
    v_hbm,
    a_hbm,
    pos,
    vol,
    dis,
    vel,
    acc,
    out_u,
    out_v,
    out_a,
    fam,
    brk,
    near_at,
    far_at,
    data,
    xrel,
    ypos,
    half,
    base,
    inv,
    w_ref,
    r_ref,
    wr_ref,
    e_ref,
    n_ref,
    col_x,
    col_y,
    col_c,
    hot_t,
    hot,
    terms,
    sum_m,
    sum_s1,
    sum_f1,
    sum_s2,
    sum_f2,
    tot1,
    tot2,
    kapq,
    coef1,
    coef2,
    disp2,
    fold_m,
    fold_s1,
    fold_f1,
    fold_s2,
    fold_f2,
    zs0,
    zsm,
    zs1,
    zs2,
    zs3,
    xs0,
    xr0,
    xsb,
    xrb,
    xsm,
    xrm,
    xs1,
    xr1,
    xs2,
    xr2,
    xs3,
    xr3,
    xs4,
    xr4,
    zf1,
    yf1,
    cf1,
    zg1,
    yg1,
    cg1,
    zf2,
    yf2,
    cf2,
    zg2,
    yg2,
    cg2,
    zf4,
    yf4,
    cf4,
    zg4,
    yg4,
    cg4,
    send_sem,
    recv_sem,
    load_sem,
):
    gx, gy, gz = lax.axis_index("gx"), lax.axis_index("gy"), lax.axis_index("gz")
    counter = [0]
    pending = []

    def there(step):
        ok = None
        for at, d in zip((gx, gy, gz), step):
            if d:
                test = at > 0 if d < 0 else at < N_DEV - 1
                ok = test if ok is None else jnp.logical_and(ok, test)
        return ok

    def target(step):
        return tuple(at + d for at, d in zip((gx, gy, gz), step))

    class Exchange:
        def __init__(self, steps, source, sink):
            self.steps, self.base = steps, counter[0]
            counter[0] += len(steps)
            self.source, self.sink = source, sink
            pending.append(self)

        def copy(self, i, step, back):
            opposite = tuple(-d for d in step)
            return pltpu.make_async_remote_copy(
                src_ref=self.source(step),
                dst_ref=self.sink(step if back else opposite),
                send_sem=send_sem.at[self.base + i],
                recv_sem=recv_sem.at[self.base + (i if back else self.steps.index(opposite))],
                device_id=target(step),
                device_id_type=pl.DeviceIdType.MESH,
            )

        def start(self):
            for i, step in enumerate(self.steps):
                pl.when(there(step))(lambda i=i, step=step: self.copy(i, step, False).start())

        def arrive(self):
            for i, step in enumerate(self.steps):
                pl.when(there(step))(lambda i=i, step=step: self.copy(i, step, True).wait_recv())

        def finish(self):
            for i, step in enumerate(self.steps):
                pl.when(there(step))(lambda i=i, step=step: self.copy(i, step, False).wait_send())

    def settle():
        while pending:
            pending.pop(0).finish()

    yz_steps = [(0, dy, dz) for dy, dz in YZ]
    diagonal_steps = [(dx, dy, dz) for dx in (-1, 1) for dy, dz in YZ]
    x_steps = [(-1, 0, 0), (1, 0, 0)]

    def fold_exchange(sums, fold):
        return Exchange(
            yz_steps,
            lambda s: sums.at[:, GHOST[s[1:]]],
            lambda s: fold.at[:, slot(s[1:])],
        )

    def add_folds(dest, sums, fold, channels):
        for c in range(channels):
            for g in range(BY * BZ):
                total = sums[c, column(g)]
                for step in YZ:
                    if g in INNER[step]:
                        first = slot(step).start + INNER[step].index(g) * 8
                        total = total + fold[c, first : first + 8]
                dest[c, column(g)] = total

    def halo_exchange(array, packed, first, last):
        def source(s):
            step = s[1:]
            if step[0] == 0:
                return packed.at[(step[1] + 1) // 2, first:last]
            groups = INNER[step]
            return array.at[first:last, groups[0] * 8 : groups[-1] * 8 + 8]

        for side in (0, 1):
            for j in range(BY):
                for c in range(first, last):
                    packed[side, c, column(j)] = array[c, column(2 * j + side)]
        return Exchange(yz_steps, source, lambda s: array.at[first:last, GHOST[s[1:]]])

    def x_exchange(send, recv, first, last):
        return Exchange(
            x_steps,
            lambda s: send.at[(s[0] + 1) // 2, first:last],
            lambda s: recv.at[(s[0] + 1) // 2, first:last],
        )

    def diagonal_exchange(send, recv):
        def of(buffers, s):
            faces_z, faces_y, corners = buffers
            x, y, z = ((d + 1) // 2 for d in s)
            if s[1] == 0:
                return faces_z.at[x, z]
            return faces_y.at[x, y] if s[2] == 0 else corners.at[x, 2 * y + z]

        return Exchange(diagonal_steps, lambda s: of(send, s), lambda s: of(recv, s))

    def pack_diagonal(send, array):
        faces_z, faces_y, corners = send
        for side in (0, 1):
            for j, x in enumerate(shared(side)):
                for i in (0, 1):
                    faces_z[side, i, j * 4 : j * 4 + 4] = array[0, pl.ds(8 * i + x, 4, stride=16), :]
                    faces_y[side, i, j * 2 : j * 2 + 2] = array[0, pl.ds(48 * i + x, 2, stride=8), :]
                for i, g in enumerate((0, 1, 6, 7)):
                    corners[side, i, j : j + 1] = array[0, pl.ds(g * 8 + x, 1), :]

    def add_diagonal(array, recv):
        faces_z, faces_y, corners = recv
        for side in (0, 1):
            for j, x in enumerate(shared(side)):
                for i, d in enumerate((-1, 1)):
                    at = pl.ds(GHOST[(0, d)].start + x, 4, stride=8)
                    array[0, at, :] = array[0, at, :] + faces_z[side, i, j * 4 : j * 4 + 4]
                    at = pl.ds(GHOST[(d, 0)].start + x, 2, stride=8)
                    array[0, at, :] = array[0, at, :] + faces_y[side, i, j * 2 : j * 2 + 2]
                for i in range(4):
                    at = pl.ds(GHOST[(i // 2 * 2 - 1, i % 2 * 2 - 1)].start + x, 1)
                    array[0, at, :] = array[0, at, :] + corners[side, i, j : j + 1]

    def shared(side):
        return ((0, 1), (BX, BX + 1))[side]

    def pack_x(send, array, channels):
        for side in (0, 1):
            for c in range(channels):
                for j, x in enumerate(shared(side)):
                    send[side, c, column(j)] = array[c, plane(x), :]

    def add_x(array, recv, channels):
        for side in (0, 1):
            for c in range(channels):
                for j, x in enumerate(shared(side)):
                    array[c, plane(x), :] = array[c, plane(x), :] + recv[side, c, column(j)]

    barrier = pltpu.get_barrier_semaphore()
    expected = jnp.int32(0)

    def greet(steps):
        for step in steps:

            @pl.when(there(step))
            def _(step=step):
                pl.semaphore_signal(
                    barrier, inc=1, device_id=target(step), device_id_type=pl.DeviceIdType.MESH
                )

    greet(x_steps)
    pairs = (
        (pos_hbm, pos),
        (vol_hbm, vol),
        (dis_hbm, dis),
        (vel_hbm, vel),
        (acc_hbm, acc),
        (fam_hbm, fam),
        (brk_hbm, brk),
        (out_u, u_hbm),
        (out_v, v_hbm),
        (out_a, a_hbm),
    )
    moves = [pltpu.make_async_copy(a, b, load_sem.at[i]) for i, (a, b) in enumerate(pairs)]
    loads, stores = moves[:7], moves[7:]
    for load in loads:
        load.start()
    greet(diagonal_steps + yz_steps)
    for step in x_steps + yz_steps + diagonal_steps:
        expected = expected + there(step).astype(jnp.int32)


    loads[0].wait()
    loads[1].wait()
    for side, x in ((0, 0), (1, BX - 1)):
        xs0[side, 3] = vol[x]
        for k in range(3):
            xs0[side, k] = pos[k, x]
    pl.semaphore_wait(barrier, expected)
    xv = x_exchange(xs0, xr0, 0, 4)
    xv.start()
    for load in loads[2:5]:
        load.wait()
    for x in (0, BX - 1, 1, 2):
        for k in range(3):
            h = vel[k, x] + 0.5 * TIME_DELTA * acc[k, x]
            u1 = dis[k, x] + TIME_DELTA * h
            data[4 + k, plane(x + 1), :] = u1
            half[k, x] = h
            base[k, plane(x + 1), :] = u1 + TIME_DELTA * h
            if x == 0 or x == BX - 1:
                xs0[x // (BX - 1), 4 + k] = u1
                xsb[x // (BX - 1), k] = u1 + TIME_DELTA * h
    xu = x_exchange(xs0, xr0, 4, 7)
    xb = x_exchange(xsb, xrb, 0, 3)
    xu.start()
    for x in range(BX):
        data[3, plane(x + 1), :] = vol[x]
        for k in range(3):
            data[k, plane(x + 1), :] = pos[k, x]

    for side, step in enumerate(x_steps):

        @pl.when(jnp.logical_not(there(step)))
        def _(side=side):
            for ref in (xr0, xrb, xrm, xr1, xr2, xr3, xr4):
                ref[side] = jnp.zeros(ref.shape[1:], jnp.float32)

    for step in diagonal_steps:

        @pl.when(jnp.logical_not(there(step)))
        def _(step=step):
            x, y, z = ((d + 1) // 2 for d in step)
            for faces_z, faces_y, corners in ((zg1, yg1, cg1), (zg2, yg2, cg2)):
                if step[1] == 0:
                    faces_z[x, z] = jnp.zeros((8, BLK), jnp.float32)
                elif step[2] == 0:
                    faces_y[x, y] = jnp.zeros((4, BLK), jnp.float32)
                else:
                    corners[x, 2 * y + z] = jnp.zeros((2, BLK), jnp.float32)
            if step[1] == 0:
                zg4[x, z] = jnp.zeros((3, 4, BLK), jnp.float32)
            elif step[2] == 0:
                yg4[x, y] = jnp.zeros((3, 2, BLK), jnp.float32)
            else:
                cg4[x, 2 * y + z] = jnp.zeros((3, 1, BLK), jnp.float32)

    for step in YZ:

        @pl.when(jnp.logical_not(there((0,) + step)))
        def _(step=step):
            for ref in (data, kapq, disp2, tot1, tot2):
                rows = GHOST[step]
                ref[:, rows] = jnp.zeros((ref.shape[0], rows.stop - rows.start, BLK), jnp.float32)
            for ref in (fold_m, fold_s1, fold_f1, fold_s2, fold_f2):
                rows = slot(step)
                ref[:, rows] = jnp.zeros((ref.shape[0], rows.stop - rows.start, BLK), jnp.float32)

    hot_t[...] = jnp.zeros_like(hot_t)
    org = [g.astype(jnp.float32) * 16.0 for g in (gx, gy, gz)]
    loads[5].wait()
    loads[6].wait()
    sub = lax.broadcasted_iota(jnp.int32, (BLK, BLK), 0)
    lane = lax.broadcasted_iota(jnp.int32, (BLK, BLK), 1)

    def row_of(block):
        x, g = block // 24, block % 24
        y, z = g // 4, g % 4
        inside_y, inside_z = (y >= 1) & (y <= BY), (z >= 1) & (z <= BZ)
        upper_y, upper_z = (y > BY).astype(jnp.int32), (z > BZ).astype(jnp.int32)
        at_y = jnp.where(inside_z, 8 + 2 * upper_y + z - 1, 20 + 2 * upper_y + upper_z)
        in_y = jnp.where(inside_z, (y - 1) * 2 + z - 1, 12 + 4 * upper_z + y - 1)
        return jnp.where(inside_y, in_y, at_y) * 8 + x

    def mask_body(t, carry):
        a, b = own[t], par[t]
        row_a, row_b = row_of(a), row_of(b)
        near_at[t] = jnp.clip(row_a // 8 * BX + row_a % 8 - 1, 0, BX * BY * BZ - 1)
        far_at[t] = jnp.clip(row_b, 0, ROWS - 1)
        apart = (a != b).astype(jnp.int32)
        live = (t < cnt[0, 0, 0]).astype(jnp.int32)
        shift = lax.broadcasted_iota(jnp.int32, (8, BLK), 0)
        rows = []
        for g in range(WORDS):
            word = fam[t, pl.ds(g, 1), :] & ~brk[t, pl.ds(g, 1), :]
            rows.append((jnp.broadcast_to(word, (8, BLK)) >> shift) & 1)
        bits = jnp.concatenate(rows, axis=0)
        bits = bits & ((sub > lane).astype(jnp.int32) | apart) & live
        w_ref[t] = bits.astype(jnp.float32).T
        code = lax.broadcasted_iota(jnp.int32, (1, BLK), 1)
        for half_at in range(2):
            hot_t[half_at, pl.ds(2 * t, 1), :] = (code + 128 * half_at == row_a).astype(jnp.float32)
            hot_t[half_at, pl.ds(2 * t + 1, 1), :] = (code + 128 * half_at == row_b).astype(
                jnp.float32
            )
        return carry

    lax.fori_loop(0, TILES, mask_body, 0, unroll=4)
    picked = jnp.concatenate([hot_t[0].T, hot_t[1].T], axis=0)[0:ROWS].astype(jnp.bfloat16)
    hot[:, 0:128] = picked
    hot[:, 128:256] = picked

    def put_columns(dest, first, values):
        def body(g, carry):
            rows = pl.ds(pl.multiple_of(g * 8, 8), 8)
            for k, value in enumerate(values(rows)):
                turned = value.T
                for x in range(BX):
                    dest[g * BX + x, first + k] = jnp.broadcast_to(
                        turned[:, x + 1 : x + 2], (BLK, BLK)
                    )
            return carry

        lax.fori_loop(0, BY * BZ, body, 0, unroll=4)

    put_columns(
        col_x, 0, lambda rows: [data[k, rows, :] - org[k] for k in range(3)] + [data[3, rows, :]]
    )

    def place_x(first, last):
        for side, x in ((0, 0), (1, BX + 1)):
            for c in range(first, last):
                data[c, plane(x), :] = xr0[side, c]

    xv.arrive()
    place_x(0, 4)
    hv = halo_exchange(data, zs0, 0, 4)
    hv.start()
    put_columns(
        col_y,
        0,
        lambda rows: [(data[k, rows, :] - org[k]) + data[4 + k, rows, :] for k in range(3)],
    )
    xu.arrive()
    place_x(4, 7)
    hu = halo_exchange(data, zs0, 4, 7)
    hu.start()
    volume = data[3, 0:OWN_ROWS]
    inv[...] = jnp.where(volume > 0.0, 1.0 / jnp.where(volume > 0.0, volume, 1.0), 0.0)
    hv.arrive()
    for k in range(3):
        xrel[k] = data[k] - org[k]
    xrel[3] = data[3]

    def far_row(ref, k, at):
        return ref[k, pl.ds(at, 1), :]

    def put_sums(t, c, values, far_sign=1):
        near = jnp.sum(values.T.reshape(16, 8, BLK), axis=0)
        far = jnp.sum(values.reshape(16, 8, BLK), axis=0)
        first = pl.multiple_of(t * 16, 16)
        terms[c, pl.ds(first, 8), :] = near
        terms[c, pl.ds(first + 8, 8), :] = far if far_sign > 0 else -far

    def gather_sums(sums, channels):
        added = []
        for c in range(channels):
            total = terms[c, pl.ds(0, 2 * TILES, stride=8), :]
            for q in range(1, 8):
                total = total + terms[c, pl.ds(q, 2 * TILES, stride=8), :]
            added.append(total)
        full = jnp.concatenate(added, axis=1)
        high = full.astype(jnp.bfloat16)
        low = (full - high.astype(jnp.float32)).astype(jnp.bfloat16)
        rest = jnp.zeros((128 - 2 * TILES, channels * 128), jnp.bfloat16)
        out = jnp.dot(
            hot[...],
            jnp.concatenate([high, rest, low, rest], axis=0),
            preferred_element_type=jnp.float32,
        )
        for c in range(channels):
            sums[c] = out[:, c * 128 : (c + 1) * 128]

    def deformed(near, at):
        d = [far_row(ypos, k, at) - col_y[near, k] for k in range(3)]
        square = jnp.maximum(d[0] * d[0] + d[1] * d[1] + d[2] * d[2], TINY)
        inverse = lax.rsqrt(square)
        return d, square * inverse, inverse

    def rest_body(t, carry):
        near, at = near_at[t], far_at[t]
        o = [far_row(xrel, k, at) - col_x[near, k] for k in range(3)]
        square = jnp.maximum(o[0] * o[0] + o[1] * o[1] + o[2] * o[2], TINY)
        rest = square * lax.rsqrt(square)
        weight = w_ref[t] * (col_x[near, 3] * far_row(xrel, 3, at))
        w_ref[t] = weight
        r_ref[t] = rest
        weighted = weight * rest
        wr_ref[t] = weighted
        put_sums(t, 0, weighted * rest)
        return carry

    def sum_body(t, carry):
        near, at = near_at[t], far_at[t]
        _, length, _ = deformed(near, at)
        put_sums(t, 0, wr_ref[t] * (length - r_ref[t]))
        return carry

    def geometry_body(known_q, t, carry):
        near, at = near_at[t], far_at[t]
        d, length, inverse = deformed(near, at)
        extension = length - r_ref[t]
        if known_q:
            extension = extension * (col_c[near, 1] + far_row(kapq, 1, at))
        e_ref[t] = extension
        scale = w_ref[t] * inverse
        for k in range(3):
            n_ref[t, k] = scale * d[k]
        return carry

    def force_body(far_p, known_q, t, carry):
        near, at = near_at[t], far_at[t]
        c = r_ref[t] * (col_c[near, 0] + far_row(far_p, 0, at))
        if known_q:
            c = c + e_ref[t]
        else:
            c = c + e_ref[t] * (col_c[near, 1] + far_row(kapq, 1, at))
        for k in range(3):
            put_sums(t, k, c * n_ref[t, k], far_sign=-1)
        return carry

    def tiles(body):
        lax.fori_loop(0, TILES, body, 0, unroll=UNROLL)

    own_rows, ghost_rows = slice(0, OWN_ROWS), slice(OWN_ROWS, ROWS)

    def total_of(tot, sums, fold, fold_way, buffers, packed, xs, xr):
        send, recv = buffers
        fold_way.arrive()
        add_folds(tot, sums, fold, 1)
        pack_x(xs, tot, 1)
        main = x_exchange(xs, xr, 0, 1)
        main.start()
        pack_diagonal(send, tot)
        diagonal = diagonal_exchange(send, recv)
        diagonal.start()
        halo = halo_exchange(tot, packed, 0, 1)
        halo.start()
        return main, diagonal, halo

    tiles(rest_body)
    gather_sums(sum_m, 1)
    fm = fold_exchange(sum_m, fold_m)
    fm.start()
    hu.arrive()
    for k in range(3):
        ypos[k] = xrel[k] + data[4 + k]
    tiles(sum_body)
    gather_sums(sum_s1, 1)
    fs = fold_exchange(sum_s1, fold_s1)
    fs.start()
    fm.arrive()
    add_folds(sum_m, sum_m, fold_m, 1)
    pack_x(xsm, sum_m, 1)
    xm = x_exchange(xsm, xrm, 0, 1)
    xm.start()
    buffers = ((zf1, yf1, cf1), (zg1, yg1, cg1))
    main, diagonal, halo = total_of(tot1, sum_s1, fold_s1, fs, buffers, zs1, xs1, xr1)
    tiles(functools.partial(geometry_body, False))
    xm.arrive()
    add_x(sum_m, xrm, 1)
    floored = jnp.maximum(sum_m[0, own_rows] * inv[...], VOLUME_FLOOR)
    kapq[0, own_rows] = (3.0 * (3.0 * K_BULK - 5.0 * MU_SHEAR)) * inv[...] / floored / floored
    kapq[1, own_rows] = 15.0 * MU_SHEAR / floored
    hm = halo_exchange(kapq, zsm, 0, 2)
    hm.start()
    put_columns(col_c, 1, lambda rows: [kapq[1, rows, :]])

    def finish_total(tot, way, recv, coef, xr, kapq_halo=None):
        main, diagonal, halo = way
        main.arrive()
        halo.finish()
        pending.remove(halo)
        add_x(tot, xr, 1)
        coef[0, own_rows] = tot[0, own_rows] * kapq[0, own_rows]
        put_columns(col_c, 0, lambda rows: [coef[0, rows, :]])
        halo.arrive()
        diagonal.arrive()
        add_diagonal(tot, recv)
        if kapq_halo is not None:
            kapq_halo.arrive()
        coef[0, ghost_rows] = tot[0, ghost_rows] * kapq[0, ghost_rows]

    finish_total(tot1, (main, diagonal, halo), buffers[1], coef1, xr1, hm)
    xb.start()

    tiles(functools.partial(force_body, coef1, False))
    gather_sums(sum_f1, 3)
    f = fold_exchange(sum_f1, fold_f1)
    f.start()
    f.arrive()
    add_folds(sum_f1, sum_f1, fold_f1, 3)
    pack_x(xs2, sum_f1, 3)
    x2 = x_exchange(xs2, xr2, 0, 3)
    x2.start()
    xb.arrive()
    for side, x in ((0, 0), (1, BX + 1)):
        for k in range(3):
            base[k, plane(x), :] = xrb[side, k]
    pending.remove(x2)
    settle()
    pending.append(x2)
    x2.arrive()
    add_x(sum_f1, xr2, 3)
    for k in range(3):
        force = sum_f1[k, own_rows] * inv[...]
        sum_f1[k, own_rows] = force
        disp2[k, own_rows] = base[k] + (TIME_DELTA * TIME_DELTA) * force
    h2 = halo_exchange(disp2, zs2, 0, 3)
    h2.start()
    put_columns(
        col_y, 0, lambda rows: [xrel[k, rows, :] + disp2[k, rows, :] for k in range(3)]
    )
    for x in range(BX):
        for k in range(3):
            half[k, x] = half[k, x] + TIME_DELTA * sum_f1[k, plane(x + 1), :]
    h2.arrive()
    for k in range(3):
        ypos[k] = xrel[k] + disp2[k]

    tiles(sum_body)
    gather_sums(sum_s2, 1)
    fs = fold_exchange(sum_s2, fold_s2)
    fs.start()
    buffers = ((zf2, yf2, cf2), (zg2, yg2, cg2))
    way = total_of(tot2, sum_s2, fold_s2, fs, buffers, zs3, xs3, xr3)
    tiles(functools.partial(geometry_body, True))
    finish_total(tot2, way, buffers[1], coef2, xr3)

    tiles(functools.partial(force_body, coef2, True))
    gather_sums(sum_f2, 3)
    for side, x in ((0, 0), (1, BX + 1)):
        for k in range(3):
            xs4[side, k] = sum_f2[k, plane(x), :]
    x4 = x_exchange(xs4, xr4, 0, 3)
    x4.start()
    for side, x in ((0, 0), (1, BX + 1)):
        for k in range(3):
            for i, d in enumerate((-1, 1)):
                at = pl.ds(GHOST[(0, d)].start + x, 4, stride=8)
                zf4[side, i, k] = sum_f2[k, at, :]
                at = pl.ds(GHOST[(d, 0)].start + x, 2, stride=8)
                yf4[side, i, k] = sum_f2[k, at, :]
            for i in range(4):
                at = pl.ds(GHOST[(i // 2 * 2 - 1, i % 2 * 2 - 1)].start + x, 1)
                cf4[side, i, k] = sum_f2[k, at, :]
    d4 = diagonal_exchange((zf4, yf4, cf4), (zg4, yg4, cg4))
    d4.start()
    f = fold_exchange(sum_f2, fold_f2)
    f.start()
    for way in (x4, d4, f):
        pending.remove(way)
    out_v[...] = half[...]
    for x in range(BX):
        for k in range(3):
            out_u[k, x] = disp2[k, plane(x + 1), :]
    stores[0].start()
    stores[1].start()
    settle()
    f.arrive()
    add_folds(sum_f2, sum_f2, fold_f2, 3)
    x4.arrive()
    d4.arrive()
    for side, x in ((0, 1), (1, BX)):
        for k in range(3):
            for i in (0, 1):
                at = pl.ds(8 * i + x, 4, stride=16)
                sum_f2[k, at, :] = sum_f2[k, at, :] + zg4[side, i, k]
                at = pl.ds(48 * i + x, 2, stride=8)
                sum_f2[k, at, :] = sum_f2[k, at, :] + yg4[side, i, k]
            for i, g in enumerate((0, 1, 6, 7)):
                at = pl.ds(g * 8 + x, 1)
                sum_f2[k, at, :] = sum_f2[k, at, :] + cg4[side, i, k]
    for x in range(BX):
        for k in range(3):
            force = sum_f2[k, plane(x + 1), :]
            if x == 0:
                force = force + xr4[0, k]
            if x == BX - 1:
                force = force + xr4[1, k]
            out_a[k, x] = force * inv[plane(x + 1), :]
    stores[2].start()
    for way in (x4, d4, f):
        way.finish()
    for store in stores:
        store.wait()


def finish_kernel(u, h, a, out_u, out_v, out_a):
    out_u[...] = u[...]
    out_v[...] = h[...] + 0.5 * TIME_DELTA * a[...]
    out_a[...] = a[...]


def per_device(
    positions,
    volume,
    displacement,
    velocity,
    acceleration,
    tile_own,
    tile_partner,
    tile_count,
    family_bits,
    broken_bits,
):
    vmem = pl.BlockSpec(memory_space=pltpu.VMEM)
    smem = pl.BlockSpec(memory_space=pltpu.SMEM)
    hbm = pl.BlockSpec(memory_space=pl.ANY)
    out = jax.ShapeDtypeStruct((3, BX, BY * BZ, BLK), jnp.float32)

    def buf(*shape, dtype=jnp.float32):
        return pltpu.VMEM(shape, dtype)

    def grid(channels):
        return buf(channels, ROWS, BLK)

    def fold(channels):
        return buf(channels, ROWS - OWN_ROWS, BLK)

    def pair(channels, rows):
        return [buf(2, channels, rows, BLK), buf(2, channels, rows, BLK)]

    def diagonals():
        return [buf(2, 2, 8, BLK), buf(2, 2, 4, BLK), buf(2, 4, 2, BLK)]

    def last_diagonals():
        return [buf(2, 2, 3, 4, BLK), buf(2, 2, 3, 2, BLK), buf(2, 4, 3, 1, BLK)]

    bits = pltpu.VMEM((TILES, WORDS, BLK), jnp.int32)
    copies = 11 * len(YZ) + 8 * 2 + 3 * 16
    points = buf(3, BX, BY * BZ, BLK)
    values = (positions, displacement, velocity, acceleration)
    pos, dis, vel, acc = (v.reshape(3, BX, BY * BZ, BLK) for v in values)
    outs = pl.pallas_call(
        kernel,
        out_shape=[out] * 3,
        in_specs=[hbm] * 5 + [smem] * 3 + [hbm] * 2,
        out_specs=[hbm] * 3,
        scratch_shapes=[
            points,
            buf(BX, BY * BZ, BLK),
            *[points] * 6,
            bits,
            bits,
            pltpu.SMEM((TILES,), jnp.int32),
            pltpu.SMEM((TILES,), jnp.int32),
            grid(7),
            grid(4),
            grid(3),
            buf(3, BX, BY * BZ, BLK),
            buf(3, OWN_ROWS, BLK),
            buf(OWN_ROWS, BLK),
            buf(TILES, BLK, BLK),
            buf(TILES, BLK, BLK),
            buf(TILES, BLK, BLK),
            buf(TILES, BLK, BLK),
            buf(TILES, 3, BLK, BLK),
            buf(BX * BY * BZ, 4, BLK, BLK),
            buf(BX * BY * BZ, 3, BLK, BLK),
            buf(BX * BY * BZ, 2, BLK, BLK),
            buf(2, 128, 128),
            buf(ROWS, 256, dtype=jnp.bfloat16),
            buf(3, TILES * 16, 128),
            grid(1),
            grid(1),
            grid(3),
            grid(1),
            grid(3),
            grid(1),
            grid(1),
            grid(2),
            grid(1),
            grid(1),
            grid(3),
            fold(1),
            fold(1),
            fold(3),
            fold(1),
            fold(3),
            buf(2, 7, BY * 8, BLK),
            buf(2, 2, BY * 8, BLK),
            buf(2, 1, BY * 8, BLK),
            buf(2, 3, BY * 8, BLK),
            buf(2, 1, BY * 8, BLK),
            *pair(7, 8),
            *pair(3, 8),
            *pair(1, 16),
            *pair(1, 16),
            *pair(3, 16),
            *pair(1, 16),
            *pair(3, 8),
            *diagonals(),
            *diagonals(),
            *diagonals(),
            *diagonals(),
            *last_diagonals(),
            *last_diagonals(),
            pltpu.SemaphoreType.DMA((copies,)),
            pltpu.SemaphoreType.DMA((copies,)),
            pltpu.SemaphoreType.DMA((10,)),
        ],
        compiler_params=pltpu.CompilerParams(
            collective_id=0, has_side_effects=True, vmem_limit_bytes=56 * 1024 * 1024
        ),
    )(
        pos,
        volume.reshape(BX, BY * BZ, BLK),
        dis,
        vel,
        acc,
        tile_own.reshape(TILES),
        tile_partner.reshape(TILES),
        tile_count,
        family_bits.reshape(TILES, WORDS, BLK),
        broken_bits.reshape(TILES, WORDS, BLK),
    )
    outs = pl.pallas_call(
        finish_kernel, out_shape=[out] * 3, in_specs=[vmem] * 3, out_specs=[vmem] * 3
    )(*outs)
    return tuple(v.reshape(3, BX, BY, BZ, BLK) for v in outs)


def solution(mesh):
    in_specs = (
        P(None, "gx", "gy", "gz", None),
        P("gx", "gy", "gz", None),
        P(None, "gx", "gy", "gz", None),
        P(None, "gx", "gy", "gz", None),
        P(None, "gx", "gy", "gz", None),
        P("gx", "gy", "gz", None),
        P("gx", "gy", "gz", None),
        P("gx", "gy", "gz"),
        P("gx", "gy", "gz", None, None, None),
        P("gx", "gy", "gz", None, None, None),
    )
    out_specs = (
        P(None, "gx", "gy", "gz", None),
        P(None, "gx", "gy", "gz", None),
        P(None, "gx", "gy", "gz", None),
    )
    return jax.shard_map(
        per_device, mesh=mesh, in_specs=in_specs, out_specs=out_specs, check_vma=False
    )
```
